256 devices in a mesh: row: 4 (over x_lo, core), col: 8 (over z), depth: 8 (over y, x_hi).
Axes of the slice: x: 4 (x_hi: 2, x_lo: 2; x = x_hi * 2 + x_lo), y: 4, z: 8, core: 2. Of those that a mesh axis runs over, the one named last changes fastest.
Arguments:
- inputs: bfloat16 [4096, 4096], P(('col', 'depth'), 'row'), may hold values from -6 to 6
- w_in: bfloat16 [4096, 16384], P('row', 'col'), may hold values from -0.09375 to 0.09375
- b_in: bfloat16 [16384], P('col'), may hold values from -4 to 4
- w_out: bfloat16 [16384, 4096], P('col', 'row'), may hold values from -0.046875 to 0.046875
- cotangent: bfloat16 [4096, 4096], P(('col', 'depth'), 'row'), may hold values from -6 to 6
Outputs:
- grad_inputs: bfloat16 [4096, 4096], P(('col', 'depth'), 'row')
- grad_w_in: float32 [4096, 16384], P(('row', 'depth'), 'col')
- grad_b_in: float32 [16384], P('col')
- grad_w_out: float32 [16384, 4096], P(('col', 'depth'), 'row')
- grad_b_out: float32 [4096], P('row')
The draws below stay inside these ranges and needn't reach their ends.
All inputs are finite; a program needn't handle non-finite values.
Results may differ from the reference program's by a relative error of at most 0.007.
Values may be sent and summed in bfloat16 or wider, within the bound.
No kernel may reach another device: no remote copies, remote signals or barrier semaphores. Data moves between devices by JAX's collectives and lax.ppermute only.
A program may use at most 128 MiB of HBM per device.

```python
import math
import jax
import jax.numpy as jnp
from jax import lax

D = 4096
F = 16384
TOKENS = 4096


def level_of(rng, extent, pieces, smallest, largest):
    def one(position, shards_of):
        draws = jax.random.uniform(jax.random.fold_in(jax.random.fold_in(rng, 6), position), (shards_of,), jnp.float32, smallest / len(pieces), largest / len(pieces))
        return jnp.repeat(jnp.exp(draws), extent[position] // shards_of).reshape((-1,) + (1,) * (len(extent) - position - 1))

    gain = one(*pieces[0])
    for cut in pieces[1:]:
        gain = gain * one(*cut)
    return gain


def normal_values(key, extent, scale, limit, shards=(), dtype=jnp.bfloat16):
    gain = level_of(key, extent, shards, -0.22, 0.18) if shards else 1.0
    array = jax.random.normal(key, extent, jnp.float32) * scale * gain
    return jnp.minimum(jnp.maximum(array, -limit), limit).astype(dtype)


def setup_inputs(seed: int = 0) -> dict:
    key_list = jax.random.split(jax.random.key(seed), 6)
    inputs = normal_values(key_list[0], (TOKENS, D), 1.0, 6.0, ((0, 64), (1, 4)))
    w_in = normal_values(key_list[1], (D, F), D ** -0.5, 0.09375, ((0, 4), (1, 8)))
    b_in = normal_values(key_list[2], (F,), 1.0, 4.0, ((0, 8),))
    w_out = normal_values(key_list[3], (F, D), F ** -0.5, 0.046875, ((0, 8), (1, 4)))
    cotangent = normal_values(key_list[4], (TOKENS, D), 1.0, 6.0, ((0, 64), (1, 4)))
    return {"inputs": inputs, "w_in": w_in, "b_in": b_in, "w_out": w_out, "cotangent": cotangent}


root_two_pi = 0.7978845608028654
cubic_coef = 0.044715

def gelu_pair(pre):
    inner = root_two_pi * (pre + cubic_coef * pre * pre * pre)
    tangent = jnp.tanh(inner)
    act = 0.5 * pre * (1.0 + tangent)
    slope = 0.5 * (1.0 + tangent) + 0.5 * pre * (1.0 - tangent * tangent) * root_two_pi * (1.0 + 3.0 * cubic_coef * pre * pre)
    return (act, slope)

def reference(inputs, w_in, b_in, w_out, cotangent):
    scale = 1.0 / math.sqrt(TOKENS)
    pre = jnp.dot(inputs, w_in, preferred_element_type=jnp.float32) + b_in.astype(jnp.float32)
    act_grad = lax.dot_general(cotangent, w_out, (((1,), (1,)), ((), ())), preferred_element_type=jnp.float32)
    act, slope = gelu_pair(pre)
    act_low = act.astype(jnp.bfloat16)
    pre_grad = (slope * act_grad).astype(jnp.bfloat16)
    grad_inputs = lax.dot_general(pre_grad, w_in, (((1,), (1,)), ((), ())), preferred_element_type=jnp.float32).astype(jnp.bfloat16)
    grad_w_in = scale * lax.dot_general(inputs, pre_grad, (((0,), (0,)), ((), ())), preferred_element_type=jnp.float32)
    grad_w_out = scale * lax.dot_general(act_low, cotangent, (((0,), (0,)), ((), ())), preferred_element_type=jnp.float32)
    grad_b_in = scale * lax.optimization_barrier(jnp.sum(pre_grad.astype(jnp.float32), axis=0))
    grad_b_out = scale * lax.optimization_barrier(jnp.sum(cotangent.astype(jnp.float32), axis=0))
    return (grad_inputs, grad_w_in, grad_b_in, grad_w_out, grad_b_out)
```

```python
import math

import jax
import jax.numpy as jnp
from jax import lax
from jax.experimental import pallas as pl
from jax.experimental.pallas import tpu as pltpu
from jax.sharding import PartitionSpec as P

root_two_pi = 0.7978845608028654
cubic_coef = 0.044715

AXES = ("row", "col", "depth")
ROWS, COLS, DEPTHS = 4, 8, 8
BF, F32 = jnp.bfloat16, jnp.float32

ORDER = ((0, 1, 6, 7, 2, 3, 4, 5), (0, 1, 2, 3, 6, 7, 4, 5))


def gelu_pair(pre):
    inner = root_two_pi * (pre + cubic_coef * pre * pre * pre)
    tangent = jnp.tanh(inner)
    act = 0.5 * pre * (1.0 + tangent)
    slope = 0.5 * (1.0 + tangent) + 0.5 * pre * (1.0 - tangent * tangent) * root_two_pi * (
        1.0 + 3.0 * cubic_coef * pre * pre
    )
    return (act, slope)


def flat(x, y, z, core):
    row = (x % 2) * 2 + core
    depth = y * 2 + x // 2
    return (row * COLS + z) * DEPTHS + depth


def pairs_of(target):
    pairs = []
    for x in range(4):
        for y in range(4):
            for z in range(8):
                for core in range(2):
                    tx, ty, tz, tc = target(x, y, z, core)
                    pairs.append((flat(x, y, z, core), flat(tx % 4, ty % 4, tz % 8, tc % 2)))
    return pairs


CORE = pairs_of(lambda x, y, z, c: (x, y, z, c ^ 1))
SWAP = pairs_of(lambda x, y, z, c: (x if x % 2 else x + 2, y, z, c))
NEAR = {
    "a": pairs_of(lambda x, y, z, c: (x ^ 1, y, z, c)),
    "r": pairs_of(lambda x, y, z, c: (x + 1 if x % 2 else x - 1, y, z, c)),
}
Y_NEXT = pairs_of(lambda x, y, z, c: (x, y ^ 1, z, c))
Y_LAST = pairs_of(lambda x, y, z, c: (x, y ^ 3, z, c))
X_HI = pairs_of(lambda x, y, z, c: (x + 2, y, z, c))
Y_ONE = [pairs_of(lambda x, y, z, c, h=h: (x, y ^ (3 if c ^ h else 1), z, c)) for h in range(2)]
Y_TWO = [pairs_of(lambda x, y, z, c, h=h: (x, y ^ (1 if c ^ h else 3), z, c)) for h in range(2)]


def send(value, pairs):
    return lax.ppermute(value, AXES, pairs)


def dot(a, b):
    return jnp.dot(a, b, preferred_element_type=F32)


def dot_t(a, b):
    return lax.dot_general(a, b, (((1,), (1,)), ((), ())), preferred_element_type=F32)


def dot_tn(a, b):
    return lax.dot_general(a, b, (((0,), (0,)), ((), ())), preferred_element_type=F32)


def plain_of(i, at):
    return (i % 8) * 2 + (at[0] ^ (i // 8))


def order_of(i, core):
    packed = [sum(k << (4 * j) for j, k in enumerate(order)) for order in ORDER]
    return (jnp.where(core == 0, packed[0], packed[1]) >> (4 * i)) & 7


def place_of(i, at):
    h = i // 8
    return (order_of(i % 8, at[0] ^ h) ^ at[1]) * 2 + (at[0] ^ h)


ANY = pl.BlockSpec(memory_space=pl.ANY)
WHOLE = pl.BlockSpec(memory_space=pltpu.VMEM)
SCALARS = pl.BlockSpec(memory_space=pltpu.SMEM)


def permute_kernel(axis, orders, at_ref, a_ref, *refs):
    outs, sems = refs[:-1], refs[-1]
    copies = []
    for o, (order, out) in enumerate(zip(orders, outs)):
        for i in range(16):
            source = pl.ds(pl.multiple_of(order(i, at_ref) * 128, 128), 128)
            target = pl.ds(i * 128, 128)
            if axis == 1:
                source, target = (slice(None), source), (slice(None), target)
            copies.append(
                pltpu.make_async_copy(a_ref.at[source], out.at[target], sems.at[16 * o + i])
            )
    for copy in copies:
        copy.start()
    for copy in copies:
        copy.wait()


def permute(at, w, axis, orders):
    return pl.pallas_call(
        lambda *refs: permute_kernel(axis, orders, *refs),
        in_specs=[SCALARS, ANY],
        out_specs=[WHOLE] * len(orders),
        out_shape=[jax.ShapeDtypeStruct(w.shape, w.dtype)] * len(orders),
        scratch_shapes=[pltpu.SemaphoreType.DMA((16 * len(orders),))],
        cost_estimate=pl.CostEstimate(flops=0, bytes_accessed=1 << 16, transcendentals=0),
        name=f"permute_{axis}",
    )(at, w)


def arrange_kernel(a_ref, tok_out, cot_out):
    n = a_ref.shape[0] // 32
    for z in range(8):
        for g in range(2):
            for i, out in enumerate((tok_out, cot_out)):
                source = (z * 4 + i * 2 + g) * n
                target = (g * 8 + z) * n
                out[target : target + n, :] = a_ref[source : source + n, :]


def arrange(gathered):
    rows, cols = gathered.shape
    return pl.pallas_call(
        arrange_kernel,
        in_specs=[WHOLE],
        out_specs=[WHOLE] * 2,
        out_shape=[jax.ShapeDtypeStruct((rows // 2, cols), BF)] * 2,
        cost_estimate=pl.CostEstimate(flops=0, bytes_accessed=1 << 16, transcendentals=0),
        name="arrange",
    )(gathered)


def gelu_kernel(chip_ref, got_a, got_r, bias_ref, act_out, slope_out):
    half = got_a.shape[0]
    for g, got in enumerate((got_a, got_r)):

        @pl.loop(0, half, step=16)
        def _(i, g=g, got=got):
            i = pl.multiple_of(i, 16)
            rows = pl.ds(pl.multiple_of(g * half + i, 16), 16)
            pre = chip_ref[rows, :].astype(F32) + got[pl.ds(i, 16), :].astype(F32)
            act, slope = gelu_pair(pre + bias_ref[...])
            act_out[rows, :] = act.astype(BF)
            slope_out[rows, :] = slope


def gelu(chip, got, bias):
    return pl.pallas_call(
        gelu_kernel,
        in_specs=[WHOLE] * 4,
        out_specs=[WHOLE] * 2,
        out_shape=[jax.ShapeDtypeStruct(chip.shape, BF), jax.ShapeDtypeStruct(chip.shape, F32)],
        cost_estimate=pl.CostEstimate(flops=0, bytes_accessed=1 << 16, transcendentals=0),
        name="gelu",
    )(chip, *got, bias)


def pre_grad_kernel(at_ref, slope_ref, chip_ref, got_a, got_r, out_ref, sum_ref):
    half = got_a.shape[0]
    for b in range(8):
        here = slice(b * 128, b * 128 + 128)
        at = pl.multiple_of((order_of(b, at_ref[0]) ^ at_ref[1]) * 128, 128)
        there = pl.ds(at, 128)
        for g, got in enumerate((got_a, got_r)):
            rows = slice(g * half, g * half + half)
            grad = chip_ref[rows, here].astype(F32) + got[:, here].astype(F32)
            value = (slope_ref[rows, here] * grad).astype(BF)
            out_ref[rows, there] = value
            sum_ref[g : g + 1, there] = jnp.sum(value.astype(F32), axis=0, keepdims=True)


def pre_grad(at, slope, chip, got):
    return pl.pallas_call(
        pre_grad_kernel,
        in_specs=[SCALARS] + [WHOLE] * 4,
        out_specs=[WHOLE] * 2,
        out_shape=[
            jax.ShapeDtypeStruct(chip.shape, BF),
            jax.ShapeDtypeStruct((2, chip.shape[1]), F32),
        ],
        cost_estimate=pl.CostEstimate(flops=0, bytes_accessed=1 << 16, transcendentals=0),
        name="pre_grad",
    )(at, slope, chip, *got)


def by_depth_kernel(at_ref, a_ref, a_out):
    for i in range(8):
        at = pl.multiple_of((order_of(i, at_ref[0]) ^ at_ref[1]) * 128, 128)
        a_out[:, i * 128 : (i + 1) * 128] = a_ref[:, pl.ds(at, 128)]


def by_depth(at, a):
    return pl.pallas_call(
        by_depth_kernel,
        in_specs=[SCALARS, WHOLE],
        out_specs=WHOLE,
        out_shape=jax.ShapeDtypeStruct(a.shape, a.dtype),
        cost_estimate=pl.CostEstimate(flops=0, bytes_accessed=1 << 16, transcendentals=0),
        name="by_depth",
    )(at, a)


def bias_kernel(at_ref, b_ref, b_out):
    for i in range(8):
        at = pl.multiple_of(place_of(i, at_ref) * 128, 128)
        b_out[:, i * 128 : (i + 1) * 128] = b_ref[:, pl.ds(at, 128)].astype(F32)


def bias_mine(at, b):
    return pl.pallas_call(
        bias_kernel,
        in_specs=[SCALARS, WHOLE],
        out_specs=WHOLE,
        out_shape=jax.ShapeDtypeStruct((1, b.shape[0] // 2), F32),
        cost_estimate=pl.CostEstimate(flops=0, bytes_accessed=1 << 14, transcendentals=0),
        name="bias_mine",
    )(at, b.reshape(1, -1))


def place_kernel(scale, at_ref, keep_ref, got_ref, keep2_ref, got2_ref, out_ref):
    for h, (k, g) in enumerate(((keep_ref, got_ref), (keep2_ref, got2_ref))):
        for i in range(8):
            at = pl.multiple_of((2 * i + (at_ref[0] ^ h)) * 128, 128)
            cols = slice(i * 128, i * 128 + 128)
            out_ref[:, pl.ds(at, 128)] = (k[:, cols] + g[:, cols].astype(F32)) * scale


def place_columns(at, scale, keep, got, keep2, got2):
    rows, cols = keep.shape
    return pl.pallas_call(
        lambda *refs: place_kernel(scale, *refs),
        in_specs=[SCALARS] + [WHOLE] * 4,
        out_specs=WHOLE,
        out_shape=jax.ShapeDtypeStruct((rows, 2 * cols), F32),
        cost_estimate=pl.CostEstimate(flops=0, bytes_accessed=1 << 16, transcendentals=0),
        name="place_columns",
    )(at, keep, got, keep2, got2)


def after(value, *others):
    return lax.optimization_barrier((value, *others))[0]


class DepthSum:
    def __init__(self, left, right, h):
        self.left, self.right, self.h = left, right, h
        self.low = lax.axis_index("depth") % 2 == 0
        self.sent = dot_tn(left[:, 512:], right).astype(BF)
        self.one = send(self.sent, Y_ONE[h])

    def second(self):
        out = dot_tn(self.left[:, 256:512], self.right) + self.one[256:].astype(F32)
        self.two = send(out.astype(BF), Y_TWO[self.h])

    def part(self, first):
        def pick(a, axis):
            low, high = lax.slice_in_dim(a, 0, 128, axis=axis), lax.slice_in_dim(a, 128, 256, axis=axis)
            return jnp.where(first, low, high)

        total = dot_tn(pick(self.left, 1), self.right) + pick(self.one, 0).astype(F32)
        return total + pick(self.two, 0).astype(F32)

    def third(self):
        self.got = send(self.part(~self.low).astype(BF), X_HI)
        self.keep = self.part(self.low)


def body(inputs, w_in, b_in, w_out, cotangent):
    core = lax.axis_index("row") % 2
    z = lax.axis_index("col")
    depth = lax.axis_index("depth")
    near = depth - depth % 2
    total_tokens = inputs.shape[0] * COLS * DEPTHS
    scale = 1.0 / math.sqrt(total_tokens)

    at = jnp.stack([core, near, z]).astype(jnp.int32)

    n = inputs.shape[0] // 2
    width = w_in.shape[1] // 2
    group = 8 * n
    far = send(jnp.concatenate([inputs[n:], cotangent[n:]], axis=0), SWAP)
    gathered = jnp.concatenate([inputs[:n], far[:n], cotangent[:n], far[n:]], axis=0)
    gathered = lax.all_gather(gathered, "col", axis=0, tiled=True)
    bias = bias_mine(at, b_in)
    w_in, w_in_plain = permute(at, w_in, 1, (place_of, plain_of))
    (w_out,) = permute(at, w_out, 0, (place_of,))
    tok, cot = arrange(gathered)

    def row_sum(mine, other):
        got = send(other.astype(BF), CORE)
        chip = (mine + got.astype(F32)).astype(BF)
        return chip, [send(chip[:group], NEAR["a"]), send(chip[group:], NEAR["r"])]

    chip, got = row_sum(dot(tok, w_in[:, :width]), dot(tok, w_in[:, width:]))
    cot_then = after(cot, chip)
    chip_two, got_two = row_sum(dot_t(cot_then, w_out[:width]), dot_t(cot_then, w_out[width:]))
    act, slope = gelu(after(chip, chip_two), got, bias)
    act_away = send(act, CORE)
    outs = [DepthSum(act, cot, 0), DepthSum(act_away, cot, 1)]

    tok_perm = by_depth(at, after(tok, outs[0].sent))
    pg, db = pre_grad(at, slope, chip_two, got_two)
    pg_away = send(pg, CORE)
    ins = [DepthSum(tok_perm, pg, 0), DepthSum(tok_perm, pg_away, 0)]
    for part in outs + ins:
        part.second()
    for part in outs + ins:
        part.third()

    pg_then = after(pg, ins[1].sent)
    gi = dot_t(pg_then, w_in_plain[:, :width]) + dot_t(pg_away, w_in_plain[:, width:])
    gi = jnp.swapaxes(gi.reshape(2, 8, n, -1), 0, 1).reshape(16 * n, -1)
    gi = lax.psum_scatter(gi, "col", scatter_dimension=0, tiled=True).astype(BF)
    grad_inputs = jnp.concatenate([gi[:n], send(gi[n:], SWAP)], axis=0)

    db = after(jnp.concatenate([db, jnp.sum(cot, axis=0, dtype=F32)[None]], axis=0), ins[1].sent)
    db = db.reshape(24, 128)
    for pairs in (Y_NEXT, Y_LAST, X_HI):
        db = db + send(db, pairs)
    db = db * scale
    grad_b_out = db[16:].reshape(-1)
    db = db[:8] + db[8:16]
    db_other = send(db, CORE)
    first = jnp.where(core == 0, db, db_other)
    second = jnp.where(core == 0, db_other, db)
    grad_b_in = jnp.concatenate([first[:, None], second[:, None]], axis=1).reshape(-1)

    one, two = ((part.keep + part.got.astype(F32)) * scale for part in outs)
    grad_w_out = jnp.concatenate(
        [jnp.where(core == 0, one, two), jnp.where(core == 0, two, one)], axis=0
    )
    grad_w_in = place_columns(at, scale, ins[0].keep, ins[0].got, ins[1].keep, ins[1].got)
    return (grad_inputs, grad_w_in, grad_b_in, grad_w_out, grad_b_out)


def solution(mesh):
    in_specs = (
        P(("col", "depth"), "row"),
        P("row", "col"),
        P("col"),
        P("col", "row"),
        P(("col", "depth"), "row"),
    )
    out_specs = (
        P(("col", "depth"), "row"),
        P(("row", "depth"), "col"),
        P("col"),
        P(("col", "depth"), "row"),
        P("row"),
    )
    return jax.shard_map(body, mesh=mesh, in_specs=in_specs, out_specs=out_specs, check_vma=False)
```

```python
import functools
import math

import jax
import jax.numpy as jnp
from jax import lax
from jax.experimental import pallas as pl
from jax.experimental.pallas import tpu as pltpu
from jax.sharding import PartitionSpec as P

root_two_pi = 0.7978845608028654
cubic_coef = 0.044715

AXES = ("row", "col", "depth")
COLS, DEPTHS = 8, 8
BF, F32 = jnp.bfloat16, jnp.float32

Y_FIRST = ((0, 1, 6, 7, 2, 3, 4, 5), (0, 1, 2, 3, 6, 7, 4, 5))
X_FIRST = ((0, 6, 2, 4, 1, 7, 3, 5), (0, 2, 6, 4, 1, 3, 7, 5))


def gelu_pair(pre):
    inner = root_two_pi * (pre + cubic_coef * pre * pre * pre)
    tangent = jnp.tanh(inner)
    act = 0.5 * pre * (1.0 + tangent)
    slope = 0.5 * (1.0 + tangent) + 0.5 * pre * (1.0 - tangent * tangent) * root_two_pi * (
        1.0 + 3.0 * cubic_coef * pre * pre
    )
    return (act, slope)


def flat(x, y, z, core):
    row = (x % 2) * 2 + core
    depth = y * 2 + x // 2
    return (row * COLS + z) * DEPTHS + depth


def pairs_of(target):
    pairs = []
    for x in range(4):
        for y in range(4):
            for z in range(8):
                for core in range(2):
                    tx, ty, tz, tc = target(x, y, z, core)
                    pairs.append((flat(x, y, z, core), flat(tx % 4, ty % 4, tz % 8, tc % 2)))
    return pairs


CORE = pairs_of(lambda x, y, z, c: (x, y, z, c ^ 1))
NEAR = pairs_of(lambda x, y, z, c: (x ^ 1, y, z, c))
X_HI = pairs_of(lambda x, y, z, c: (x + 2, y, z, c))
Y_ONE = pairs_of(lambda x, y, z, c: (x, y ^ (3 if c else 1), z, c))
Y_TWO = pairs_of(lambda x, y, z, c: (x, y ^ (1 if c else 3), z, c))
Z = {k: pairs_of(lambda x, y, z, c, k=k: (x, y, z + k, c)) for k in (-2, -1, 1, 2)}
Z_XOR = {k: pairs_of(lambda x, y, z, c, k=k: (x, y, z ^ k, c)) for k in (1, 2, 4)}


def send(value, pairs):
    return lax.ppermute(value, AXES, pairs)


def together(*values):
    return lax.optimization_barrier(values)


def after(value, *others):
    return together(value, *others)[0]


def dot(a, b):
    return jnp.dot(a, b, preferred_element_type=F32)


def dot_t(a, b):
    return lax.dot_general(a, b, (((1,), (1,)), ((), ())), preferred_element_type=F32)


def dot_tn(a, b):
    return lax.dot_general(a, b, (((0,), (0,)), ((), ())), preferred_element_type=F32)


ANY = pl.BlockSpec(memory_space=pl.ANY)
WHOLE = pl.BlockSpec(memory_space=pltpu.VMEM)
SCALARS = pl.BlockSpec(memory_space=pltpu.SMEM)
STEP = 256


def tiles(n):
    return [slice(i, i + STEP) for i in range(0, n, STEP)]


def local(kernel, name, outs, at, *arrays):
    single = not isinstance(outs, list)
    shapes = [jax.ShapeDtypeStruct(*out) for out in ([outs] if single else outs)]
    return pl.pallas_call(
        kernel,
        in_specs=[SCALARS] + [WHOLE] * len(arrays),
        out_specs=WHOLE if single else [WHOLE] * len(shapes),
        out_shape=shapes[0] if single else shapes,
        cost_estimate=pl.CostEstimate(flops=0, bytes_accessed=1 << 12, transcendentals=0),
        compiler_params=pltpu.CompilerParams(vmem_limit_bytes=16 << 20),
        name=name,
    )(at, *arrays)


def order_of(i, at, order=Y_FIRST):
    packed = [sum(k << (4 * j) for j, k in enumerate(ks)) for ks in order]
    return ((jnp.where(at[0] == 0, packed[0], packed[1]) >> (4 * i)) & 7) ^ at[1]


def place_of(i, at):
    h = i // 8
    return order_of(i % 8, (at[0] ^ h, at[1])) * 2 + (at[0] ^ h)


def plain_of(i, at):
    return (i % 8) * 2 + (at[0] ^ (i // 8))


def permute_kernel(axis, orders, at_ref, a_ref, *refs):
    outs, sems = refs[:-1], refs[-1]
    copies = []
    for o, (order, out) in enumerate(zip(orders, outs)):
        for i in range(16):
            source = pl.ds(pl.multiple_of(order(i, at_ref) * 128, 128), 128)
            target = pl.ds(i * 128, 128)
            if axis == 1:
                source, target = (slice(None), source), (slice(None), target)
            copies.append(
                pltpu.make_async_copy(a_ref.at[source], out.at[target], sems.at[16 * o + i])
            )
    for copy in copies:
        copy.start()
    for copy in copies:
        copy.wait()


def permute(at, w, axis, orders):
    return pl.pallas_call(
        functools.partial(permute_kernel, axis, orders),
        in_specs=[SCALARS, ANY],
        out_specs=[WHOLE] * len(orders),
        out_shape=[jax.ShapeDtypeStruct(w.shape, w.dtype)] * len(orders),
        scratch_shapes=[pltpu.SemaphoreType.DMA((16 * len(orders),))],
        compiler_params=pltpu.CompilerParams(vmem_limit_bytes=16 << 20),
        cost_estimate=pl.CostEstimate(flops=0, bytes_accessed=1 << 12, transcendentals=0),
        name=f"permute_{axis}",
    )(at, w)


def bias_kernel(at_ref, b_ref, b_out):
    for i in range(8):
        at = pl.multiple_of(place_of(i, at_ref) * 128, 128)
        b_out[:, i * 128 : (i + 1) * 128] = b_ref[:, pl.ds(at, 128)].astype(F32)


def bias_mine(at, b):
    return local(bias_kernel, "bias_mine", ((1, b.shape[0] // 2), F32), at, b.reshape(1, -1))


def pack_kernel(a_ref, b_ref, out_ref, sems):
    rows = a_ref.shape[0]
    copies = [
        pltpu.make_async_copy(ref, out_ref.at[pl.ds(i * rows, rows)], sems.at[i])
        for i, ref in enumerate((a_ref, b_ref))
    ]
    for copy in copies:
        copy.start()
    for copy in copies:
        copy.wait()


def pack(a, b):
    return pl.pallas_call(
        pack_kernel,
        in_specs=[ANY] * 2,
        out_specs=WHOLE,
        out_shape=jax.ShapeDtypeStruct((2 * a.shape[0], a.shape[1]), a.dtype),
        scratch_shapes=[pltpu.SemaphoreType.DMA((2,))],
        cost_estimate=pl.CostEstimate(flops=0, bytes_accessed=1 << 12, transcendentals=0),
        name="pack",
    )(a, b)


AWAY_Z = (0, 1, 2, -2, -1, 3, -3, 4)
NEAR_BLOCKS = 5


def gather_near(block, *meanwhile):
    near = [send(block, Z[-k]) for k in AWAY_Z[1:NEAR_BLOCKS]]
    return [block, *together(*near, *meanwhile)[:4]]


def gather_far(near):
    half = near[0].shape[0] // 2
    up, down = near[2], near[3]
    last = send(up[:half], Z[-2]), send(down[half:], Z[2])
    return [send(up, Z[-1]), send(down, Z[1]), *last]


def arrange_near_kernel(at_ref, *refs):
    blocks, w_ref, tok_out, out_ref = refs[:NEAR_BLOCKS], *refs[NEAR_BLOCKS:]
    n = blocks[0].shape[0] // 2
    for i, block in enumerate(blocks):
        tok_out[i * n : (i + 1) * n, :] = block[:n, :]
    width = out_ref.shape[1]
    for cols in tiles(width):
        other = slice(width + cols.start, width + cols.stop)
        out_ref[:, cols] = dot(tok_out[...], w_ref[:, other]).astype(BF)


def arrange_near(at, blocks, w_in):
    rows, cols = blocks[0].shape
    rows = rows // 2 * NEAR_BLOCKS
    outs = [((rows, cols), BF), ((rows, w_in.shape[1] // 2), BF)]
    return local(arrange_near_kernel, "arrange_near", outs, at, *blocks, w_in)


def arrange_far_kernel(at_ref, tok_ref, *refs):
    blocks, w_ref, tok_out, cot_out, out_ref, sums, sum_out = refs[:9], *refs[9:]
    n = blocks[0].shape[0] // 2
    first = tok_ref.shape[0]
    tok_out[:first, :] = tok_ref[...]
    for i, block in enumerate(blocks[:7]):
        rows = slice(i * n, (i + 1) * n)
        if i >= NEAR_BLOCKS:
            tok_out[rows, :] = block[:n, :]
        cot_out[rows, :] = block[n:, :]
    tok_out[7 * n :, :] = blocks[7][...]
    cot_out[7 * n :, :] = blocks[8][...]
    width = out_ref.shape[1]
    for cols in tiles(width):
        other = slice(width + cols.start, width + cols.stop)
        out_ref[:, cols] = dot(tok_out[first:, :], w_ref[:, other]).astype(BF)
    for i, k in enumerate(AWAY_Z):
        value = jnp.sum(cot_out[i * n : (i + 1) * n, :].astype(F32), axis=0, keepdims=True)
        sums[pl.ds((at_ref[2] + k) & 7, 1), :] = value
    sum_out[...] = jnp.sum(sums[...], axis=0, keepdims=True)


def arrange_far(at, tok, blocks, w_in):
    rows, cols = blocks[0].shape
    rows, width = 4 * rows, w_in.shape[1] // 2
    outs = [((rows, cols), BF)] * 2 + [((rows - tok.shape[0], width), BF), ((8, cols), F32), ((1, cols), F32)]
    tok, cot, terms, _, cot_sum = local(arrange_far_kernel, "arrange_far", outs, at, tok, *blocks, w_in)
    return tok, cot, terms, cot_sum


def grad_other_kernel(at_ref, cot_ref, w_ref, out_ref):
    width = out_ref.shape[1]
    for cols in tiles(width):
        other = slice(width + cols.start, width + cols.stop)
        out_ref[:, cols] = dot_t(cot_ref[...], w_ref[other, :]).astype(BF)


def grad_other(at, cot, w_out):
    out = ((cot.shape[0], w_out.shape[0] // 2), BF)
    return local(grad_other_kernel, "grad_other", out, at, cot, w_out)


def chip_kernel(transposed, at_ref, a_ref, w_ref, got_ref, out_ref):
    rows = slice(a_ref.shape[0] - out_ref.shape[0], a_ref.shape[0])
    for cols in tiles(out_ref.shape[1]):
        if transposed:
            value = dot_t(a_ref[rows, :], w_ref[cols, :])
        else:
            value = dot(a_ref[rows, :], w_ref[:, cols])
        out_ref[:, cols] = (value + got_ref[:, cols].astype(F32)).astype(BF)


def chip_sum(at, a, w, got, transposed):
    kernel = functools.partial(chip_kernel, transposed)
    return local(kernel, "chip_sum", (got.shape, BF), at, a, w, got)


def gelu_kernel(slope, at_ref, *refs):
    halves, bias_ref, out_ref = (refs[:2], refs[2:4]), refs[4], refs[5]
    base = 0
    for chip_ref, got_ref in halves:

        @pl.loop(0, chip_ref.shape[0], step=16)
        def _(i, base=base, chip_ref=chip_ref, got_ref=got_ref):
            i = pl.multiple_of(i, 16)
            rows = pl.ds(i, 16)
            pre = chip_ref[rows, :].astype(F32) + got_ref[rows, :].astype(F32)
            value = gelu_pair(pre + bias_ref[...])[slope]
            out_ref[pl.ds(pl.multiple_of(base + i, 16), 16), :] = value.astype(out_ref.dtype)

        base += chip_ref.shape[0]


def gelu(at, near, far, bias, slope):
    rows = near[0].shape[0] + far[0].shape[0]
    out, name = ((rows, bias.shape[1]), F32 if slope else BF), "slope" if slope else "act"
    return local(functools.partial(gelu_kernel, slope), name, out, at, *near, *far, bias)


def pre_grad_kernel(at_ref, slope_ref, chip_ref, got_ref, out_ref, sum_ref):
    for b in range(8):
        here = slice(b * 128, b * 128 + 128)
        there = pl.ds(pl.multiple_of(order_of(b, at_ref) * 128, 128), 128)
        grad = chip_ref[:, here].astype(F32) + got_ref[:, here].astype(F32)
        value = (slope_ref[:, here] * grad).astype(BF)
        out_ref[:, there] = value
        sum_ref[:, there] = jnp.sum(value.astype(F32), axis=0, keepdims=True)


def pre_grad(at, slope, chip, got):
    outs = [(slope.shape, BF), ((1, slope.shape[1]), F32)]
    return local(pre_grad_kernel, "pre_grad", outs, at, slope, chip, got)


def by_depth_kernel(at_ref, a_ref, *outs):
    for order, out in zip((Y_FIRST, X_FIRST), outs):
        for i in range(8):
            at = pl.multiple_of(order_of(i, at_ref, order) * 128, 128)
            out[:, i * 128 : (i + 1) * 128] = a_ref[:, pl.ds(at, 128)]


def by_depth(at, a):
    return local(by_depth_kernel, "by_depth", [(a.shape, a.dtype)] * 2, at, a)


OWN = (((512, 1024),), ((256, 512),), ((128, 256),), ((0, 128),))
AWAY = (((256, 512), (768, 1024)), ((512, 768),), ((128, 256),), ((0, 128),))


def split(value):
    high = value.astype(BF).astype(F32)
    return jnp.concatenate([high, value - high], axis=0).astype(BF)


def joined(ref, start):
    return ref[start : start + 8, :].astype(F32) + ref[start + 8 : start + 16, :].astype(F32)


SIZES = (512, 256, 128, 128)


def depth_kernel(level, sides, at_ref, *refs):
    count = min(level, 2)
    lefts, right_ref, refs = refs[: len(sides)], refs[len(sides)], refs[len(sides) + 1 :]
    got_refs, refs, out_ref = refs[:count], refs[count:-1], refs[-1]
    size = SIZES[level]
    skip = 0 if level == 3 else size
    for s, (side, left_ref) in enumerate(zip(sides, lefts)):
        done = 0
        for start, stop in side[level]:
            rows = slice(s * size + done, s * size + done + stop - start)
            for cols in tiles(out_ref.shape[1]):
                value = dot_tn(left_ref[:, start:stop], right_ref[:, cols])
                for i, got_ref in enumerate(got_refs):
                    base = s * SIZES[i] + skip + done
                    value = value + got_ref[base : base + stop - start, cols].astype(F32)
                out_ref[rows, cols] = value.astype(out_ref.dtype)
            done += stop - start
    if refs and level == 0:
        own, away, cot_sum = refs
        row = lax.broadcasted_iota(jnp.int32, (8, out_ref.shape[1]), 0)
        value = jnp.where(row == 2, cot_sum[...], 0.0)
        value = jnp.where(row == at_ref[0], own[...], value)
        value = jnp.where(row == 1 - at_ref[0], away[...], value)
        out_ref[512:528, :] = split(value)
    elif refs and level == 1:
        out_ref[256:272, :] = split(joined(refs[0], 512) + joined(got_refs[0], 512))
    elif refs and level == 2:
        out_ref[128:144, :] = refs[0][256:272, :]
        out_ref[144:160, :] = got_refs[1][256:272, :]


class DepthSum:
    def __init__(self, at, sides, lefts, right, pairs, riders=()):
        self.at, self.sides, self.lefts, self.right, self.pairs = at, sides, lefts, right, pairs
        self.riders, self.got, self.sent = riders, [], []

    def rows(self, level, dtype, riders):
        size = SIZES[level] * len(self.sides) + (0, 16, 32)[bool(riders) + (bool(riders) and level == 2)]
        kernel = functools.partial(depth_kernel, level, self.sides)
        out = ((size, self.right.shape[1]), dtype)
        got = self.got[: min(level, 2)]
        return local(
            kernel, f"depth_{level}", out, self.at, *self.lefts, self.right, *got, *riders
        )

    def exchange(self):
        level = len(self.got)
        riders = self.riders if level == 0 else self.sent[-1:] if self.riders else ()
        self.sent.append(self.rows(level, BF, riders))
        self.got.append(send(self.sent[-1], self.pairs[level]))

    def kept_rows(self, *earlier):
        self.right = after(self.right, *earlier)
        return self.rows(3, F32, ())


def inputs_grad_kernel(at_ref, own_ref, away_ref, w_ref, out_ref, sent_ref):
    n = out_ref.shape[0] // 8
    width = own_ref.shape[1]
    for cols in tiles(out_ref.shape[1]):
        value = dot_t(own_ref[...], w_ref[cols, :width]) + dot_t(away_ref[...], w_ref[cols, width:])
        for i, away in enumerate(AWAY_Z):
            k = at_ref[2] ^ ((at_ref[2] + away) & 7)
            place = ((k & 1) << 2) | (k & 2) | (k >> 2)
            out_ref[pl.ds(pl.multiple_of(place * n, n), n), cols] = value[i * n : (i + 1) * n]
    sent_ref[...] = out_ref[4 * n :, :].astype(BF)


def inputs_grad(at, own, away, w_in):
    rows, cols = own.shape[0], w_in.shape[0]
    outs = [((rows, cols), F32), ((rows // 2, cols), BF)]
    return local(inputs_grad_kernel, "inputs_grad", outs, at, own, away, w_in)


def rows_kernel(scale, at_ref, keep_ref, got_ref, out_ref):
    for h in range(2):
        here = slice(h * 128, h * 128 + 128)
        there = pl.ds(pl.multiple_of((at_ref[0] ^ h) * 128, 128), 128)
        out_ref[there, :] = (keep_ref[here, :] + got_ref[here, :].astype(F32)) * scale


def place_rows(at, scale, keep, got):
    kernel = functools.partial(rows_kernel, scale)
    return local(kernel, "place_rows", (keep.shape, F32), at, keep, got)


def columns_kernel(scale, at_ref, keep_ref, got_ref, keep2_ref, got2_ref, sent_ref, out_ref, bias_ref):
    for h, (k, g) in enumerate(((keep_ref, got_ref), (keep2_ref, got2_ref))):
        for i in range(8):
            at = pl.multiple_of((2 * i + (at_ref[0] ^ h)) * 128, 128)
            cols = slice(i * 128, i * 128 + 128)
            out_ref[:, pl.ds(at, 128)] = (k[:, cols] + g[:128, cols].astype(F32)) * scale
    v = [joined(ref, start) for ref in (sent_ref, got2_ref) for start in (128, 144)]
    zero = at_ref[0] == 0
    first = v[0] + jnp.where(zero, v[1], v[2])
    second = jnp.where(zero, v[2], v[1]) + v[3]
    total = (first + second) * scale
    for i in range(8):
        cols = slice(i * 128, i * 128 + 128)
        for row in range(2):
            bias_ref[2 * i + row : 2 * i + row + 1, :] = total[row : row + 1, cols]
        bias_ref[16 + i : 17 + i, :] = total[2:3, cols]


def place_columns(at, scale, keep, got, keep2, got2, sent2):
    rows, cols = keep.shape
    kernel = functools.partial(columns_kernel, scale)
    outs = [((rows, 2 * cols), F32), ((24, 128), F32)]
    return local(kernel, "place_columns", outs, at, keep, got, keep2, got2, sent2)


def body(inputs, w_in, b_in, w_out, cotangent):
    core = lax.axis_index("row") % 2
    total_tokens = inputs.shape[0] * COLS * DEPTHS
    scale = 1.0 / math.sqrt(total_tokens)
    at = jnp.stack([core, lax.axis_index("depth"), lax.axis_index("col")]).astype(jnp.int32)
    n = inputs.shape[0]

    bias = bias_mine(at, b_in)
    w_in, w_in_plain = permute(at, w_in, 1, (place_of, plain_of))
    (w_out,) = permute(at, w_out, 0, (place_of,))
    near = gather_near(pack(inputs, cotangent), bias, w_in_plain, w_out)
    far = gather_far(near)

    tok_near, terms = arrange_near(at, near, w_in)
    chip_near = chip_sum(at, tok_near, w_in, send(terms, CORE), False)
    got_near = send(chip_near, NEAR)
    tok, cot, terms, cot_sum = arrange_far(at, tok_near, near + far, w_in)
    terms, got_near = together(send(terms, CORE), got_near)
    chip_far = chip_sum(at, tok, w_in, terms, False)
    got_far = send(chip_far, NEAR)
    terms = grad_other(at, after(cot, chip_far), w_out)
    chip_two = chip_sum(at, cot, w_out, send(terms, CORE), True)
    got_two = send(chip_two, NEAR)
    got_far = after(got_far, chip_two)
    act = gelu(at, (chip_near, got_near), (chip_far, got_far), bias, 0)
    act_away = send(act, CORE)

    out = DepthSum(at, (OWN, AWAY), (act, act_away), cot, (Y_ONE, Y_TWO, X_HI))
    out.exchange()
    bias = after(bias, act_away)
    slope = gelu(at, (chip_near, got_near), (chip_far, got_far), bias, 1)
    tok_one, tok_two = by_depth(at, after(tok, slope))
    pg, db = pre_grad(at, after(slope, tok_one), chip_two, got_two)
    pg_away = send(pg, CORE)
    db_away = send(db, CORE)

    out.got[0], tok_one, tok_two = together(out.got[0], tok_one, tok_two, pg)[:3]
    out.exchange()
    one = DepthSum(at, (OWN,), (after(tok_one, out.sent[1]),), pg, (Y_ONE, Y_TWO, X_HI))
    one.exchange()
    riders = db, db_away, cot_sum
    two = DepthSum(at, (OWN,), (tok_two,), pg_away, (X_HI, Y_ONE, Y_TWO), riders)
    two.exchange()
    gi, gi_sent = inputs_grad(at, after(pg, one.sent[0], two.sent[0]), pg_away, w_in_plain)
    gi_got = [send(gi_sent, Z_XOR[1])]

    one.got[0], two.got[0], out.got[1], gi_got[0] = together(
        one.got[0], two.got[0], out.got[1], gi_got[0]
    )
    one.exchange()
    two.exchange()
    out.exchange()
    gi_sent = (gi[2 * n : 4 * n] + gi_got[0][2 * n :].astype(F32)).astype(BF)
    gi_got.append(send(gi_sent, Z_XOR[2]))
    out_kept = out.kept_rows(one.sent[1], two.sent[1], out.sent[2], gi_sent)

    one.got[1], two.got[1], out.got[2], gi_got[1] = together(
        one.got[1], two.got[1], out.got[2], gi_got[1]
    )
    one.exchange()
    two.exchange()
    gi_sent = gi[n : 2 * n] + gi_got[0][n : 2 * n].astype(F32) + gi_got[1][n:].astype(F32)
    gi_sent = gi_sent.astype(BF)
    gi_got.append(send(gi_sent, Z_XOR[4]))
    sent = one.sent[2], two.sent[2], gi_sent
    one_kept, two_kept = one.kept_rows(*sent), two.kept_rows(*sent)
    grad_w_out = place_rows(at, scale, after(out_kept, one_kept, two_kept), out.got[2])
    gi = gi[:n] + sum(got[:n].astype(F32) for got in gi_got)
    grad_inputs = gi.astype(BF)
    grad_w_in, db = place_columns(
        at, scale, one_kept, one.got[2], two_kept, two.got[2], two.sent[2]
    )
    grad_b_in, grad_b_out = db[:16].reshape(-1), db[16:].reshape(-1)
    return (grad_inputs, grad_w_in, grad_b_in, grad_w_out, grad_b_out)


def solution(mesh):
    in_specs = (
        P(("col", "depth"), "row"),
        P("row", "col"),
        P("col"),
        P("col", "row"),
        P(("col", "depth"), "row"),
    )
    out_specs = (
        P(("col", "depth"), "row"),
        P(("row", "depth"), "col"),
        P("col"),
        P(("col", "depth"), "row"),
        P("row"),
    )
    return jax.shard_map(body, mesh=mesh, in_specs=in_specs, out_specs=out_specs, check_vma=False)
```

```python
import functools
import math

import jax
import jax.numpy as jnp
from jax import lax
from jax.experimental import pallas as pl
from jax.experimental.pallas import tpu as pltpu
from jax.sharding import PartitionSpec as P

root_two_pi = 0.7978845608028654
cubic_coef = 0.044715

AXES = ("row", "col", "depth")
COLS, DEPTHS = 8, 8
BF, F32 = jnp.bfloat16, jnp.float32

Y_FIRST = ((0, 1, 6, 7, 2, 3, 4, 5), (0, 1, 2, 3, 6, 7, 4, 5))
X_FIRST = ((0, 6, 2, 4, 1, 7, 3, 5), (0, 2, 6, 4, 1, 3, 7, 5))


def gelu_pair(pre):
    inner = root_two_pi * (pre + cubic_coef * pre * pre * pre)
    tangent = jnp.tanh(inner)
    act = 0.5 * pre * (1.0 + tangent)
    slope = 0.5 * (1.0 + tangent) + 0.5 * pre * (1.0 - tangent * tangent) * root_two_pi * (
        1.0 + 3.0 * cubic_coef * pre * pre
    )
    return (act, slope)


def flat(x, y, z, core):
    row = (x % 2) * 2 + core
    depth = y * 2 + x // 2
    return (row * COLS + z) * DEPTHS + depth


def pairs_of(target):
    pairs = []
    for x in range(4):
        for y in range(4):
            for z in range(8):
                for core in range(2):
                    tx, ty, tz, tc = target(x, y, z, core)
                    pairs.append((flat(x, y, z, core), flat(tx % 4, ty % 4, tz % 8, tc % 2)))
    return pairs


CORE = pairs_of(lambda x, y, z, c: (x, y, z, c ^ 1))
NEAR = pairs_of(lambda x, y, z, c: (x ^ 1, y, z, c))
X_HI = pairs_of(lambda x, y, z, c: (x + 2, y, z, c))
Y_ONE = pairs_of(lambda x, y, z, c: (x, y ^ (3 if c else 1), z, c))
Y_TWO = pairs_of(lambda x, y, z, c: (x, y ^ (1 if c else 3), z, c))
Z = {k: pairs_of(lambda x, y, z, c, k=k: (x, y, z + k, c)) for k in (-2, -1, 1, 2)}
Z_STEPS = [
    pairs_of(lambda x, y, z, c, k=k: (x, y, z + (k if (z + c) % 2 == 0 else -k), c)) for k in (1, -1, 3)
]
Z_ORDER = (0, 3, 7, 4, 1, 6, 2, 5)


def send(value, pairs):
    return lax.ppermute(value, AXES, pairs)


def together(*values):
    return lax.optimization_barrier(values)


def after(value, *others):
    return together(value, *others)[0]


def dot(a, b):
    return jnp.dot(a, b, preferred_element_type=F32)


def dot_t(a, b):
    return lax.dot_general(a, b, (((1,), (1,)), ((), ())), preferred_element_type=F32)


def dot_tn(a, b):
    return lax.dot_general(a, b, (((0,), (0,)), ((), ())), preferred_element_type=F32)


ANY = pl.BlockSpec(memory_space=pl.ANY)
WHOLE = pl.BlockSpec(memory_space=pltpu.VMEM)
SCALARS = pl.BlockSpec(memory_space=pltpu.SMEM)
STEP = 256


def tiles(n):
    return [slice(i, i + STEP) for i in range(0, n, STEP)]


def local(kernel, name, outs, at, *arrays):
    single = not isinstance(outs, list)
    shapes = [jax.ShapeDtypeStruct(*out) for out in ([outs] if single else outs)]
    return pl.pallas_call(
        kernel,
        in_specs=[SCALARS] + [WHOLE] * len(arrays),
        out_specs=WHOLE if single else [WHOLE] * len(shapes),
        out_shape=shapes[0] if single else shapes,
        cost_estimate=pl.CostEstimate(flops=0, bytes_accessed=1 << 12, transcendentals=0),
        compiler_params=pltpu.CompilerParams(vmem_limit_bytes=16 << 20),
        name=name,
    )(at, *arrays)


def order_of(i, at, order=Y_FIRST):
    packed = [sum(k << (4 * j) for j, k in enumerate(ks)) for ks in order]
    return ((jnp.where(at[0] == 0, packed[0], packed[1]) >> (4 * i)) & 7) ^ at[1]


def place_of(i, at):
    h = i // 8
    return order_of(i % 8, (at[0] ^ h, at[1])) * 2 + (at[0] ^ h)


def plain_of(i, at):
    return (i % 8) * 2 + (at[0] ^ (i // 8))


def permute_kernel(axis, orders, at_ref, a_ref, *refs):
    outs, sems = refs[:-1], refs[-1]
    copies = []
    for o, (order, out) in enumerate(zip(orders, outs)):
        for i in range(16):
            source = pl.ds(pl.multiple_of(order(i, at_ref) * 128, 128), 128)
            target = pl.ds(i * 128, 128)
            if axis == 1:
                source, target = (slice(None), source), (slice(None), target)
            copies.append(
                pltpu.make_async_copy(a_ref.at[source], out.at[target], sems.at[16 * o + i])
            )
    for copy in copies:
        copy.start()
    for copy in copies:
        copy.wait()


def permute(at, w, axis, orders):
    return pl.pallas_call(
        functools.partial(permute_kernel, axis, orders),
        in_specs=[SCALARS, ANY],
        out_specs=[WHOLE] * len(orders),
        out_shape=[jax.ShapeDtypeStruct(w.shape, w.dtype)] * len(orders),
        scratch_shapes=[pltpu.SemaphoreType.DMA((16 * len(orders),))],
        compiler_params=pltpu.CompilerParams(vmem_limit_bytes=16 << 20),
        cost_estimate=pl.CostEstimate(flops=0, bytes_accessed=1 << 12, transcendentals=0),
        name=f"permute_{axis}",
    )(at, w)


def bias_kernel(at_ref, b_ref, b_out):
    for i in range(8):
        at = pl.multiple_of(place_of(i, at_ref) * 128, 128)
        b_out[:, i * 128 : (i + 1) * 128] = b_ref[:, pl.ds(at, 128)].astype(F32)


def bias_mine(at, b):
    return local(bias_kernel, "bias_mine", ((1, b.shape[0] // 2), F32), at, b.reshape(1, -1))


def pack_kernel(a_ref, b_ref, out_ref, sems):
    rows = a_ref.shape[0]
    copies = [
        pltpu.make_async_copy(ref, out_ref.at[pl.ds(i * rows, rows)], sems.at[i])
        for i, ref in enumerate((a_ref, b_ref))
    ]
    for copy in copies:
        copy.start()
    for copy in copies:
        copy.wait()


def pack(a, b):
    return pl.pallas_call(
        pack_kernel,
        in_specs=[ANY] * 2,
        out_specs=WHOLE,
        out_shape=jax.ShapeDtypeStruct((2 * a.shape[0], a.shape[1]), a.dtype),
        scratch_shapes=[pltpu.SemaphoreType.DMA((2,))],
        cost_estimate=pl.CostEstimate(flops=0, bytes_accessed=1 << 12, transcendentals=0),
        name="pack",
    )(a, b)


AWAY_Z = (0, 1, 2, -2, -1, 3, -3, 4)
NEAR_BLOCKS = 5


def gather_near(block, *meanwhile):
    near = [send(block, Z[-k]) for k in AWAY_Z[1:NEAR_BLOCKS]]
    return [block, *together(*near, *meanwhile)[:4]]


def gather_far(near):
    half = near[0].shape[0] // 2
    up, down = near[2], near[3]
    last = send(up[:half], Z[-2]), send(down[half:], Z[2])
    return [send(up, Z[-1]), send(down, Z[1]), *last]


def arrange_near_kernel(at_ref, *refs):
    blocks, w_ref, tok_out, out_ref = refs[:NEAR_BLOCKS], *refs[NEAR_BLOCKS:]
    n = blocks[0].shape[0] // 2
    for i, block in enumerate(blocks):
        tok_out[i * n : (i + 1) * n, :] = block[:n, :]
    width = out_ref.shape[1]
    for cols in tiles(width):
        other = slice(width + cols.start, width + cols.stop)
        out_ref[:, cols] = dot(tok_out[...], w_ref[:, other]).astype(BF)


def arrange_near(at, blocks, w_in):
    rows, cols = blocks[0].shape
    rows = rows // 2 * NEAR_BLOCKS
    outs = [((rows, cols), BF), ((rows, w_in.shape[1] // 2), BF)]
    return local(arrange_near_kernel, "arrange_near", outs, at, *blocks, w_in)


def arrange_far_kernel(at_ref, tok_ref, *refs):
    blocks, w_ref, tok_out, cot_out, out_ref, sums, sum_out = refs[:9], *refs[9:]
    n = blocks[0].shape[0] // 2
    first = tok_ref.shape[0]
    tok_out[:first, :] = tok_ref[...]
    for i, block in enumerate(blocks[:7]):
        rows = slice(i * n, (i + 1) * n)
        if i >= NEAR_BLOCKS:
            tok_out[rows, :] = block[:n, :]
        cot_out[rows, :] = block[n:, :]
    tok_out[7 * n :, :] = blocks[7][...]
    cot_out[7 * n :, :] = blocks[8][...]
    width = out_ref.shape[1]
    for cols in tiles(width):
        other = slice(width + cols.start, width + cols.stop)
        out_ref[:, cols] = dot(tok_out[first:, :], w_ref[:, other]).astype(BF)
    for i, k in enumerate(AWAY_Z):
        value = jnp.sum(cot_out[i * n : (i + 1) * n, :].astype(F32), axis=0, keepdims=True)
        sums[pl.ds((at_ref[2] + k) & 7, 1), :] = value
    sum_out[...] = jnp.sum(sums[...], axis=0, keepdims=True)


def arrange_far(at, tok, blocks, w_in):
    rows, cols = blocks[0].shape
    rows, width = 4 * rows, w_in.shape[1] // 2
    outs = [((rows, cols), BF)] * 2 + [((rows - tok.shape[0], width), BF), ((8, cols), F32), ((1, cols), F32)]
    tok, cot, terms, _, cot_sum = local(arrange_far_kernel, "arrange_far", outs, at, tok, *blocks, w_in)
    return tok, cot, terms, cot_sum


def grad_other_kernel(at_ref, cot_ref, w_ref, out_ref):
    width = out_ref.shape[1]
    for cols in tiles(width):
        other = slice(width + cols.start, width + cols.stop)
        out_ref[:, cols] = dot_t(cot_ref[...], w_ref[other, :]).astype(BF)


def grad_other(at, cot, w_out):
    out = ((cot.shape[0], w_out.shape[0] // 2), BF)
    return local(grad_other_kernel, "grad_other", out, at, cot, w_out)


def chip_kernel(transposed, at_ref, a_ref, w_ref, got_ref, out_ref):
    rows = slice(a_ref.shape[0] - out_ref.shape[0], a_ref.shape[0])
    for cols in tiles(out_ref.shape[1]):
        if transposed:
            value = dot_t(a_ref[rows, :], w_ref[cols, :])
        else:
            value = dot(a_ref[rows, :], w_ref[:, cols])
        out_ref[:, cols] = (value + got_ref[:, cols].astype(F32)).astype(BF)


def chip_sum(at, a, w, got, transposed):
    kernel = functools.partial(chip_kernel, transposed)
    return local(kernel, "chip_sum", (got.shape, BF), at, a, w, got)


def gelu_kernel(slope, at_ref, *refs):
    halves, bias_ref, out_ref = (refs[:2], refs[2:4]), refs[4], refs[5]
    base = 0
    for chip_ref, got_ref in halves:

        @pl.loop(0, chip_ref.shape[0], step=16)
        def _(i, base=base, chip_ref=chip_ref, got_ref=got_ref):
            i = pl.multiple_of(i, 16)
            rows = pl.ds(i, 16)
            pre = chip_ref[rows, :].astype(F32) + got_ref[rows, :].astype(F32)
            value = gelu_pair(pre + bias_ref[...])[slope]
            out_ref[pl.ds(pl.multiple_of(base + i, 16), 16), :] = value.astype(out_ref.dtype)

        base += chip_ref.shape[0]


def gelu(at, near, far, bias, slope):
    rows = near[0].shape[0] + far[0].shape[0]
    out, name = ((rows, bias.shape[1]), F32 if slope else BF), "slope" if slope else "act"
    return local(functools.partial(gelu_kernel, slope), name, out, at, *near, *far, bias)


def split(value):
    high = value.astype(BF).astype(F32)
    return jnp.concatenate([high, value - high], axis=0).astype(BF)


def joined(ref, start):
    return ref[start : start + 8, :].astype(F32) + ref[start + 8 : start + 16, :].astype(F32)


def pre_grad_kernel(at_ref, slope_ref, chip_ref, got_ref, out_ref):
    tokens = chip_ref.shape[0]
    row = lax.broadcasted_iota(jnp.int32, (8, 128), 0)
    for b in range(8):
        here = slice(b * 128, b * 128 + 128)
        there = pl.ds(pl.multiple_of(order_of(b, at_ref) * 128, 128), 128)
        grad = chip_ref[:, here].astype(F32) + got_ref[:, here].astype(F32)
        value = (slope_ref[:, here] * grad).astype(BF)
        out_ref[:tokens, there] = value
        total = jnp.sum(value.astype(F32), axis=0, keepdims=True)
        out_ref[tokens:, there] = split(jnp.where(row == 0, total, 0.0))


def pre_grad(at, slope, chip, got):
    rows, cols = slope.shape
    return local(pre_grad_kernel, "pre_grad", ((rows + 16, cols), BF), at, slope, chip, got)


def by_depth_kernel(at_ref, a_ref, *outs):
    for order, out in zip((Y_FIRST[::-1], X_FIRST), outs):
        for i in range(8):
            at = pl.multiple_of(order_of(i, at_ref, order) * 128, 128)
            out[:, i * 128 : (i + 1) * 128] = a_ref[:, pl.ds(at, 128)]


def by_depth(at, a):
    return local(by_depth_kernel, "by_depth", [(a.shape, a.dtype)] * 2, at, a)


OWN = (((512, 1024),), ((256, 512),), ((128, 256),), ((0, 128),))
AWAY = (((256, 512), (768, 1024)), ((512, 768),), ((128, 256),), ((0, 128),))


SIZES = (512, 256, 128, 128)


def depth_part(plan, at_ref, refs, out_ref):
    sides, level = plan["sides"], plan["level"]
    lefts = [next(refs) for _ in sides]
    right_ref = next(refs)
    got_refs = [(next(refs), offset) for offset in plan["got"]]
    size, base = SIZES[level], plan["base"]
    skip = 0 if level == 3 else size
    for s, (side, left_ref) in enumerate(zip(sides, lefts)):
        done = 0
        for start, stop in side[level]:
            rows = slice(base + s * size + done, base + s * size + done + stop - start)
            for cols in tiles(out_ref.shape[1]):
                value = dot_tn(left_ref[:, start:stop], right_ref[: left_ref.shape[0], cols])
                for i, (got_ref, offset) in enumerate(got_refs):
                    at = offset + s * SIZES[i] + skip + done
                    value = value + got_ref[at : at + stop - start, cols].astype(F32)
                out_ref[rows, cols] = value.astype(out_ref.dtype)
            done += stop - start
    base += size * len(sides)
    if plan["riders"] == "first":
        own, away, cot_sum = next(refs), next(refs), next(refs)
        row = lax.broadcasted_iota(jnp.int32, (8, out_ref.shape[1]), 0)
        value = jnp.where(row == 2, cot_sum[...], 0.0)
        value = jnp.where(row == at_ref[0], joined(own, own.shape[0] - 16)[:1], value)
        value = jnp.where(row == 1 - at_ref[0], joined(away, away.shape[0] - 16)[:1], value)
        out_ref[base : base + 16, :] = split(value)
    elif plan["riders"] is not None:
        sent, got = next(refs), got_refs[-1]
        here, there = plan["riders"] + SIZES[level - 1], got[1] + SIZES[level - 1]
        if level == 1:
            out_ref[base : base + 16, :] = split(joined(sent, here) + joined(got[0], there))
        else:
            out_ref[base : base + 16, :] = sent[here : here + 16, :]
            out_ref[base + 16 : base + 32, :] = got[0][there : there + 16, :]


def depth_kernel(plans, at_ref, *refs):
    given = iter(refs[:-1])
    for plan in plans:
        depth_part(plan, at_ref, given, refs[-1])


class DepthSum:
    def __init__(self, sides, lefts, right, riders=()):
        self.sides, self.lefts, self.right, self.riders = sides, lefts, right, riders
        self.sent, self.got = [], []

    def plan(self, level, base):
        got, riders, size = self.got[: min(level, 2)], None, SIZES[level] * len(self.sides)
        given = [*self.lefts, self.right, *(message for message, _ in got)]
        if self.riders and level < 3:
            riders = self.sent[-1][1] if level else "first"
            given += [self.sent[-1][0]] if level else self.riders
            size += 32 if level == 2 else 16
        offsets = [offset for _, offset in got]
        return dict(sides=self.sides, level=level, got=offsets, riders=riders, base=base), given, size

    def kept_rows(self, at, *earlier):
        self.right = after(self.right, *earlier)
        plan, given, size = self.plan(3, 0)
        out = ((size, self.right.shape[1]), F32)
        return local(functools.partial(depth_kernel, [plan]), "depth_kept", out, at, *given)


def exchange(at, parts, pairs):
    plans, operands, base = [], [], 0
    for part in parts:
        plan, given, size = part.plan(len(part.got), base)
        plans.append(plan)
        operands += given
        base += size
    out = ((base, parts[0].right.shape[1]), BF)
    message = local(functools.partial(depth_kernel, plans), "depth", out, at, *operands)
    got = send(message, pairs)
    for part, plan in zip(parts, plans):
        part.sent.append((message, plan["base"]))
        part.got.append((got, plan["base"]))
    return message, got


def arrived(parts, got):
    for part in parts:
        part.got[-1] = got, part.got[-1][1]


def inputs_grad_kernel(at_ref, own_ref, away_ref, w_ref, out_ref, sent_ref):
    tokens, width = out_ref.shape[0], own_ref.shape[1]
    n = tokens // 8
    for cols in tiles(out_ref.shape[1]):
        value = dot_t(own_ref[:tokens, :], w_ref[cols, :width])
        value = value + dot_t(away_ref[:tokens, :], w_ref[cols, width:])
        for i, away in enumerate(AWAY_Z):
            place = jnp.where((at_ref[2] + at_ref[0]) % 2 == 0, Z_ORDER.index(away % 8), Z_ORDER.index(-away % 8))
            out_ref[pl.ds(pl.multiple_of(place * n, n), n), cols] = value[i * n : (i + 1) * n]
    sent_ref[...] = out_ref[4 * n :, :].astype(BF)


def inputs_grad(at, own, away, w_in):
    rows, cols = own.shape[0] - 16, w_in.shape[0]
    outs = [((rows, cols), F32), ((rows // 2, cols), BF)]
    return local(inputs_grad_kernel, "inputs_grad", outs, at, own, away, w_in)


def rows_kernel(scale, at_ref, keep_ref, got_ref, out_ref):
    for h in range(2):
        here = slice(h * 128, h * 128 + 128)
        there = pl.ds(pl.multiple_of((at_ref[0] ^ h) * 128, 128), 128)
        out_ref[there, :] = (keep_ref[here, :] + got_ref[here, :].astype(F32)) * scale


def place_rows(at, scale, keep, got):
    kernel = functools.partial(rows_kernel, scale)
    return local(kernel, "place_rows", (keep.shape, F32), at, keep, got)


def columns_kernel(scale, at_ref, keep_ref, got_ref, keep2_ref, got2_ref, sent_ref, out_ref, in_ref, bias_ref):
    for h, (k, g) in enumerate(((keep_ref, got_ref), (keep2_ref, got2_ref))):
        for i in range(8):
            at = pl.multiple_of((2 * i + (at_ref[0] ^ h)) * 128, 128)
            cols = slice(i * 128, i * 128 + 128)
            out_ref[:, pl.ds(at, 128)] = (k[:, cols] + g[:128, cols].astype(F32)) * scale
    v = [joined(ref, start) for ref in (sent_ref, got2_ref) for start in (128, 144)]
    zero = at_ref[0] == 0
    first = v[0] + jnp.where(zero, v[1], v[2])
    second = jnp.where(zero, v[2], v[1]) + v[3]
    total = (first + second) * scale
    for i in range(8):
        cols = slice(i * 128, i * 128 + 128)
        for row in range(2):
            in_ref[2 * i + row : 2 * i + row + 1, :] = total[row : row + 1, cols]
        bias_ref[i : i + 1, :] = total[2:3, cols]


def place_columns(at, scale, keep, got, keep2, got2, sent2):
    rows, cols = keep.shape
    kernel = functools.partial(columns_kernel, scale)
    outs = [((rows, 2 * cols), F32), ((16, 128), F32), ((8, 128), F32)]
    return local(kernel, "place_columns", outs, at, keep, got, keep2, got2, sent2)


def body(inputs, w_in, b_in, w_out, cotangent):
    core = lax.axis_index("row") % 2
    total_tokens = inputs.shape[0] * COLS * DEPTHS
    scale = 1.0 / math.sqrt(total_tokens)
    at = jnp.stack([core, lax.axis_index("depth"), lax.axis_index("col")]).astype(jnp.int32)
    n = inputs.shape[0]

    bias = bias_mine(at, b_in)
    w_in, w_in_plain = permute(at, w_in, 1, (place_of, plain_of))
    (w_out,) = permute(at, w_out, 0, (place_of,))
    near = gather_near(pack(inputs, cotangent), bias, w_in_plain, w_out)
    far = gather_far(near)

    tok_near, terms = arrange_near(at, near, w_in)
    chip_near = chip_sum(at, tok_near, w_in, send(terms, CORE), False)
    got_near = send(chip_near, NEAR)
    tok, cot, terms, cot_sum = arrange_far(at, tok_near, near + far, w_in)
    terms, got_near = together(send(terms, CORE), got_near)
    chip_far = chip_sum(at, tok, w_in, terms, False)
    got_far = send(chip_far, NEAR)
    terms = grad_other(at, after(cot, got_far), w_out)
    chip_two = chip_sum(at, cot, w_out, send(terms, CORE), True)
    got_two = send(chip_two, NEAR)
    act = gelu(at, (chip_near, got_near), (chip_far, got_far), bias, 0)
    act_away = send(act, CORE)

    out = DepthSum((OWN, AWAY), (act, act_away), cot)
    _, got = exchange(at, [out], Y_ONE)
    bias = after(bias, act_away)
    slope = gelu(at, (chip_near, got_near), (chip_far, got_far), bias, 1)
    tok_one, tok_two = by_depth(at, after(tok, slope))
    pg = pre_grad(at, after(slope, tok_one), chip_two, got_two)
    pg_away = send(pg, CORE)

    got, tok_one, tok_two, _ = together(got, tok_one, tok_two, pg)
    arrived([out], got)
    one = DepthSum((OWN,), (tok_one,), pg)
    sent_one, got_one = exchange(at, [out, one], Y_TWO)
    two = DepthSum((OWN,), (after(tok_two, sent_one),), pg_away, (pg, pg_away, cot_sum))
    sent_two, got_two = exchange(at, [two], X_HI)
    gi, gi_sent = inputs_grad(at, after(pg, sent_two), pg_away, w_in_plain)
    gi_got = [send(gi_sent, Z_STEPS[0])]
    gi_sent = (gi[2 * n : 4 * n] + gi_got[0][2 * n :].astype(F32)).astype(BF)
    gi_got.append(send(gi_sent, Z_STEPS[1]))

    got_one, got_two, gi_got[1] = together(got_one, got_two, gi_got[1])
    arrived([out, one], got_one)
    arrived([two], got_two)
    sent_one, got_one = exchange(at, [one, two], Y_ONE)
    sent_two, got_two = exchange(at, [out], X_HI)
    gi_sent = gi[n : 2 * n] + gi_got[0][n : 2 * n].astype(F32) + gi_got[1][n:].astype(F32)
    gi_sent = gi_sent.astype(BF)
    gi_got.append(send(gi_sent, Z_STEPS[2]))
    out_kept = out.kept_rows(at, sent_one, sent_two, gi_sent)

    got_one, got_two, gi_got[2], out_kept = together(got_one, got_two, gi_got[2], out_kept)
    arrived([one, two], got_one)
    arrived([out], got_two)
    sent_one, got_one = exchange(at, [one], X_HI)
    sent_two, got_two = exchange(at, [two], Y_TWO)
    sent = sent_one, sent_two
    one_kept, two_kept = one.kept_rows(at, *sent), two.kept_rows(at, *sent)
    grad_w_out = place_rows(at, scale, after(out_kept, one_kept, two_kept), out.got[2][0])
    gi = gi[:n] + sum(got[:n].astype(F32) for got in gi_got)
    grad_inputs = gi.astype(BF)
    grad_w_in, db_in, db_out = place_columns(
        at, scale, one_kept, got_one, two_kept, got_two, sent_two
    )
    grad_b_in, grad_b_out = db_in.reshape(-1), db_out.reshape(-1)
    return (grad_inputs, grad_w_in, grad_b_in, grad_w_out, grad_b_out)


def solution(mesh):
    in_specs = (
        P(("col", "depth"), "row"),
        P("row", "col"),
        P("col"),
        P("col", "row"),
        P(("col", "depth"), "row"),
    )
    out_specs = (
        P(("col", "depth"), "row"),
        P(("row", "depth"), "col"),
        P("col"),
        P(("col", "depth"), "row"),
        P("row"),
    )
    return jax.shard_map(body, mesh=mesh, in_specs=in_specs, out_specs=out_specs, check_vma=False)
```

```python
import functools
import math

import jax
import jax.numpy as jnp
from jax import lax
from jax.experimental import pallas as pl
from jax.experimental.pallas import tpu as pltpu
from jax.sharding import PartitionSpec as P

root_two_pi = 0.7978845608028654
cubic_coef = 0.044715

AXES = ("row", "col", "depth")
COLS, DEPTHS = 8, 8
BF, F32 = jnp.bfloat16, jnp.float32

Y_FIRST = ((0, 1, 6, 7, 2, 3, 4, 5), (0, 1, 2, 3, 6, 7, 4, 5))
X_FIRST = ((0, 6, 2, 4, 1, 7, 3, 5), (0, 2, 6, 4, 1, 3, 7, 5))


def gelu_pair(pre):
    inner = root_two_pi * (pre + cubic_coef * pre * pre * pre)
    tangent = jnp.tanh(inner)
    act = 0.5 * pre * (1.0 + tangent)
    slope = 0.5 * (1.0 + tangent) + 0.5 * pre * (1.0 - tangent * tangent) * root_two_pi * (
        1.0 + 3.0 * cubic_coef * pre * pre
    )
    return (act, slope)


def flat(x, y, z, core):
    row = (x % 2) * 2 + core
    depth = y * 2 + x // 2
    return (row * COLS + z) * DEPTHS + depth


def pairs_of(target):
    pairs = []
    for x in range(4):
        for y in range(4):
            for z in range(8):
                for core in range(2):
                    tx, ty, tz, tc = target(x, y, z, core)
                    pairs.append((flat(x, y, z, core), flat(tx % 4, ty % 4, tz % 8, tc % 2)))
    return pairs


CORE = pairs_of(lambda x, y, z, c: (x, y, z, c ^ 1))
NEAR = pairs_of(lambda x, y, z, c: (x ^ 1, y, z, c))
X_HI = pairs_of(lambda x, y, z, c: (x + 2, y, z, c))
Y_ONE = pairs_of(lambda x, y, z, c: (x, y ^ (3 if c else 1), z, c))
Y_TWO = pairs_of(lambda x, y, z, c: (x, y ^ (1 if c else 3), z, c))
Z = {k: pairs_of(lambda x, y, z, c, k=k: (x, y, z + k, c)) for k in (-2, -1, 1, 2)}
Z_STEPS = [
    pairs_of(lambda x, y, z, c, k=k: (x, y, z + (k if (z + c) % 2 == 0 else -k), c)) for k in (1, -1, 3)
]
Z_ORDER = (0, 3, 7, 4, 1, 6, 2, 5)


def send(value, pairs):
    return lax.ppermute(value, AXES, pairs)


def together(*values):
    return lax.optimization_barrier(values)


def after(value, *others):
    return together(value, *others)[0]


def dot(a, b):
    return jnp.dot(a, b, preferred_element_type=F32)


def dot_t(a, b):
    return lax.dot_general(a, b, (((1,), (1,)), ((), ())), preferred_element_type=F32)


def dot_tn(a, b):
    return lax.dot_general(a, b, (((0,), (0,)), ((), ())), preferred_element_type=F32)


ANY = pl.BlockSpec(memory_space=pl.ANY)
WHOLE = pl.BlockSpec(memory_space=pltpu.VMEM)
SCALARS = pl.BlockSpec(memory_space=pltpu.SMEM)
STEP = 256


def tiles(n):
    return [slice(i, i + STEP) for i in range(0, n, STEP)]


def local(kernel, name, outs, at, *arrays):
    single = not isinstance(outs, list)
    shapes = [jax.ShapeDtypeStruct(*out) for out in ([outs] if single else outs)]
    return pl.pallas_call(
        kernel,
        in_specs=[SCALARS] + [WHOLE] * len(arrays),
        out_specs=WHOLE if single else [WHOLE] * len(shapes),
        out_shape=shapes[0] if single else shapes,
        cost_estimate=pl.CostEstimate(flops=0, bytes_accessed=1 << 12, transcendentals=0),
        compiler_params=pltpu.CompilerParams(vmem_limit_bytes=16 << 20),
        name=name,
    )(at, *arrays)


def order_of(i, at, order=Y_FIRST):
    packed = [sum(k << (4 * j) for j, k in enumerate(ks)) for ks in order]
    return ((jnp.where(at[0] == 0, packed[0], packed[1]) >> (4 * i)) & 7) ^ at[1]


def place_of(i, at):
    h = i // 8
    return order_of(i % 8, (at[0] ^ h, at[1])) * 2 + (at[0] ^ h)


def plain_of(i, at):
    return (i % 8) * 2 + (at[0] ^ (i // 8))


def permute_kernel(axis, orders, at_ref, a_ref, *refs):
    outs, sems = refs[:-1], refs[-1]
    copies = []
    for o, (order, out) in enumerate(zip(orders, outs)):
        for i in range(16):
            source = pl.ds(pl.multiple_of(order(i, at_ref) * 128, 128), 128)
            target = pl.ds(i * 128, 128)
            if axis == 1:
                source, target = (slice(None), source), (slice(None), target)
            copies.append(
                pltpu.make_async_copy(a_ref.at[source], out.at[target], sems.at[16 * o + i])
            )
    for copy in copies:
        copy.start()
    for copy in copies:
        copy.wait()


def permute(at, w, axis, orders):
    return pl.pallas_call(
        functools.partial(permute_kernel, axis, orders),
        in_specs=[SCALARS, ANY],
        out_specs=[WHOLE] * len(orders),
        out_shape=[jax.ShapeDtypeStruct(w.shape, w.dtype)] * len(orders),
        scratch_shapes=[pltpu.SemaphoreType.DMA((16 * len(orders),))],
        compiler_params=pltpu.CompilerParams(vmem_limit_bytes=16 << 20),
        cost_estimate=pl.CostEstimate(flops=0, bytes_accessed=1 << 12, transcendentals=0),
        name=f"permute_{axis}",
    )(at, w)


def bias_kernel(at_ref, b_ref, b_out):
    for i in range(8):
        at = pl.multiple_of(place_of(i, at_ref) * 128, 128)
        b_out[:, i * 128 : (i + 1) * 128] = b_ref[:, pl.ds(at, 128)].astype(F32)


def bias_mine(at, b):
    return local(bias_kernel, "bias_mine", ((1, b.shape[0] // 2), F32), at, b.reshape(1, -1))


def pack_kernel(a_ref, b_ref, out_ref, sems):
    rows = a_ref.shape[0]
    copies = [
        pltpu.make_async_copy(ref, out_ref.at[pl.ds(i * rows, rows)], sems.at[i])
        for i, ref in enumerate((a_ref, b_ref))
    ]
    for copy in copies:
        copy.start()
    for copy in copies:
        copy.wait()


def pack(a, b):
    return pl.pallas_call(
        pack_kernel,
        in_specs=[ANY] * 2,
        out_specs=WHOLE,
        out_shape=jax.ShapeDtypeStruct((2 * a.shape[0], a.shape[1]), a.dtype),
        scratch_shapes=[pltpu.SemaphoreType.DMA((2,))],
        cost_estimate=pl.CostEstimate(flops=0, bytes_accessed=1 << 12, transcendentals=0),
        name="pack",
    )(a, b)


AWAY_Z = (0, 1, 2, -2, -1, 3, -3, 4)
NEAR_BLOCKS = 5


def gather_near(block, *meanwhile):
    near = [send(block, Z[-k]) for k in AWAY_Z[1:NEAR_BLOCKS]]
    return [block, *together(*near, *meanwhile)[:4]]


def gather_far(near):
    half = near[0].shape[0] // 2
    up, down = near[2], near[3]
    last = send(up[:half], Z[-2]), send(down[half:], Z[2])
    return [send(up, Z[-1]), send(down, Z[1]), *last]


def arrange_near_kernel(at_ref, *refs):
    blocks, w_ref, tok_out, out_ref = refs[:NEAR_BLOCKS], *refs[NEAR_BLOCKS:]
    n = blocks[0].shape[0] // 2
    for i, block in enumerate(blocks):
        tok_out[i * n : (i + 1) * n, :] = block[:n, :]
    width = out_ref.shape[1]
    for cols in tiles(width):
        other = slice(width + cols.start, width + cols.stop)
        out_ref[:, cols] = dot(tok_out[...], w_ref[:, other]).astype(BF)


def arrange_near(at, blocks, w_in):
    rows, cols = blocks[0].shape
    rows = rows // 2 * NEAR_BLOCKS
    outs = [((rows, cols), BF), ((rows, w_in.shape[1] // 2), BF)]
    return local(arrange_near_kernel, "arrange_near", outs, at, *blocks, w_in)


def arrange_far_kernel(at_ref, tok_ref, *refs):
    blocks, w_ref, tok_out, cot_out, out_ref, sums, sum_out = refs[:9], *refs[9:]
    n = blocks[0].shape[0] // 2
    first = tok_ref.shape[0]
    tok_out[:first, :] = tok_ref[...]
    for i, block in enumerate(blocks[:7]):
        rows = slice(i * n, (i + 1) * n)
        if i >= NEAR_BLOCKS:
            tok_out[rows, :] = block[:n, :]
        cot_out[rows, :] = block[n:, :]
    tok_out[7 * n :, :] = blocks[7][...]
    cot_out[7 * n :, :] = blocks[8][...]
    width = out_ref.shape[1]
    for cols in tiles(width):
        other = slice(width + cols.start, width + cols.stop)
        out_ref[:, cols] = dot(tok_out[first:, :], w_ref[:, other]).astype(BF)
    for i, k in enumerate(AWAY_Z):
        value = jnp.sum(cot_out[i * n : (i + 1) * n, :].astype(F32), axis=0, keepdims=True)
        sums[pl.ds((at_ref[2] + k) & 7, 1), :] = value
    sum_out[...] = jnp.sum(sums[...], axis=0, keepdims=True)


def arrange_far(at, tok, blocks, w_in):
    rows, cols = blocks[0].shape
    rows, width = 4 * rows, w_in.shape[1] // 2
    outs = [((rows, cols), BF)] * 2 + [((rows - tok.shape[0], width), BF), ((8, cols), F32), ((1, cols), F32)]
    tok, cot, terms, _, cot_sum = local(arrange_far_kernel, "arrange_far", outs, at, tok, *blocks, w_in)
    return tok, cot, terms, cot_sum


def grad_other_kernel(at_ref, cot_ref, w_ref, out_ref):
    width = out_ref.shape[1]
    for cols in tiles(width):
        other = slice(width + cols.start, width + cols.stop)
        out_ref[:, cols] = dot_t(cot_ref[...], w_ref[other, :]).astype(BF)


def grad_other(at, cot, w_out):
    out = ((cot.shape[0], w_out.shape[0] // 2), BF)
    return local(grad_other_kernel, "grad_other", out, at, cot, w_out)


def chip_kernel(transposed, at_ref, a_ref, w_ref, got_ref, out_ref):
    rows = slice(a_ref.shape[0] - out_ref.shape[0], a_ref.shape[0])
    for cols in tiles(out_ref.shape[1]):
        if transposed:
            value = dot_t(a_ref[rows, :], w_ref[cols, :])
        else:
            value = dot(a_ref[rows, :], w_ref[:, cols])
        out_ref[:, cols] = (value + got_ref[:, cols].astype(F32)).astype(BF)


def chip_sum(at, a, w, got, transposed):
    kernel = functools.partial(chip_kernel, transposed)
    return local(kernel, "chip_sum", (got.shape, BF), at, a, w, got)


def gelu_kernel(slope, at_ref, *refs):
    halves, bias_ref, out_ref = (refs[:2], refs[2:4]), refs[4], refs[5]
    base = 0
    for chip_ref, got_ref in halves:

        @pl.loop(0, chip_ref.shape[0], step=16)
        def _(i, base=base, chip_ref=chip_ref, got_ref=got_ref):
            i = pl.multiple_of(i, 16)
            rows = pl.ds(i, 16)
            pre = chip_ref[rows, :].astype(F32) + got_ref[rows, :].astype(F32)
            value = gelu_pair(pre + bias_ref[...])[slope]
            out_ref[pl.ds(pl.multiple_of(base + i, 16), 16), :] = value.astype(out_ref.dtype)

        base += chip_ref.shape[0]


def gelu(at, near, far, bias, slope):
    rows = near[0].shape[0] + far[0].shape[0]
    out, name = ((rows, bias.shape[1]), F32 if slope else BF), "slope" if slope else "act"
    return local(functools.partial(gelu_kernel, slope), name, out, at, *near, *far, bias)


def split(value):
    high = value.astype(BF).astype(F32)
    return jnp.concatenate([high, value - high], axis=0).astype(BF)


def joined(ref, start):
    return ref[start : start + 8, :].astype(F32) + ref[start + 8 : start + 16, :].astype(F32)


def pre_grad_kernel(at_ref, slope_ref, chip_ref, got_ref, out_ref):
    tokens = chip_ref.shape[0]
    row = lax.broadcasted_iota(jnp.int32, (8, 128), 0)
    for b in range(8):
        here = slice(b * 128, b * 128 + 128)
        there = pl.ds(pl.multiple_of(order_of(b, at_ref) * 128, 128), 128)
        grad = chip_ref[:, here].astype(F32) + got_ref[:, here].astype(F32)
        value = (slope_ref[:, here] * grad).astype(BF)
        out_ref[:tokens, there] = value
        total = jnp.sum(value.astype(F32), axis=0, keepdims=True)
        out_ref[tokens:, there] = split(jnp.where(row == 0, total, 0.0))


def pre_grad(at, slope, chip, got):
    rows, cols = slope.shape
    return local(pre_grad_kernel, "pre_grad", ((rows + 16, cols), BF), at, slope, chip, got)


def by_depth_kernel(at_ref, a_ref, *outs):
    for order, out in zip((Y_FIRST[::-1], X_FIRST), outs):
        for i in range(8):
            at = pl.multiple_of(order_of(i, at_ref, order) * 128, 128)
            out[:, i * 128 : (i + 1) * 128] = a_ref[:, pl.ds(at, 128)]


def by_depth(at, a):
    return local(by_depth_kernel, "by_depth", [(a.shape, a.dtype)] * 2, at, a)


OWN = (((512, 1024),), ((256, 512),), ((128, 256),), ((0, 128),))
AWAY = (((256, 512), (768, 1024)), ((512, 768),), ((128, 256),), ((0, 128),))


SIZES = (512, 256, 128, 128)


def depth_part(plan, at_ref, refs, out_ref):
    sides, level = plan["sides"], plan["level"]
    lefts = [next(refs) for _ in sides]
    right_ref = next(refs)
    got_refs = [(next(refs), offset) for offset in plan["got"]]
    size, base = SIZES[level], plan["base"]
    skip = 0 if level == 3 else size
    for s, (side, left_ref) in enumerate(zip(sides, lefts)):
        done = 0
        for start, stop in side[level]:
            rows = slice(base + s * size + done, base + s * size + done + stop - start)
            for cols in tiles(out_ref.shape[1]):
                value = dot_tn(left_ref[:, start:stop], right_ref[: left_ref.shape[0], cols])
                for i, (got_ref, offset) in enumerate(got_refs):
                    at = offset + s * SIZES[i] + skip + done
                    value = value + got_ref[at : at + stop - start, cols].astype(F32)
                out_ref[rows, cols] = value.astype(out_ref.dtype)
            done += stop - start
    base += size * len(sides)
    if plan["riders"] == "first":
        own, away, cot_sum = next(refs), next(refs), next(refs)
        row = lax.broadcasted_iota(jnp.int32, (8, out_ref.shape[1]), 0)
        value = jnp.where(row == 2, cot_sum[...], 0.0)
        value = jnp.where(row == at_ref[0], joined(own, own.shape[0] - 16)[:1], value)
        value = jnp.where(row == 1 - at_ref[0], joined(away, away.shape[0] - 16)[:1], value)
        out_ref[base : base + 16, :] = split(value)
    elif plan["riders"] is not None:
        sent, got = next(refs), got_refs[-1]
        here, there = plan["riders"] + SIZES[level - 1], got[1] + SIZES[level - 1]
        if level == 1:
            out_ref[base : base + 16, :] = split(joined(sent, here) + joined(got[0], there))
        else:
            out_ref[base : base + 16, :] = sent[here : here + 16, :]
            out_ref[base + 16 : base + 32, :] = got[0][there : there + 16, :]


def depth_kernel(plans, at_ref, *refs):
    given = iter(refs[:-1])
    for plan in plans:
        depth_part(plan, at_ref, given, refs[-1])


class DepthSum:
    def __init__(self, sides, lefts, right, riders=()):
        self.sides, self.lefts, self.right, self.riders = sides, lefts, right, riders
        self.sent, self.got = [], []

    def plan(self, level, base):
        got, riders, size = self.got[: min(level, 2)], None, SIZES[level] * len(self.sides)
        given = [*self.lefts, self.right, *(message for message, _ in got)]
        if self.riders and level < 3:
            riders = self.sent[-1][1] if level else "first"
            given += [self.sent[-1][0]] if level else self.riders
            size += 32 if level == 2 else 16
        offsets = [offset for _, offset in got]
        return dict(sides=self.sides, level=level, got=offsets, riders=riders, base=base), given, size


def kept_rows(at, parts, *earlier):
    plans, operands, base = [], [], 0
    parts[0].right = after(parts[0].right, *earlier)
    for part in parts:
        plan, given, size = part.plan(3, base)
        plans.append(plan)
        operands += given
        base += size
    out = ((base, parts[0].right.shape[1]), F32)
    return local(functools.partial(depth_kernel, plans), "depth_kept", out, at, *operands)


def exchange(at, parts, pairs):
    plans, operands, base = [], [], 0
    for part in parts:
        plan, given, size = part.plan(len(part.got), base)
        plans.append(plan)
        operands += given
        base += size
    out = ((base, parts[0].right.shape[1]), BF)
    message = local(functools.partial(depth_kernel, plans), "depth", out, at, *operands)
    got = send(message, pairs)
    for part, plan in zip(parts, plans):
        part.sent.append((message, plan["base"]))
        part.got.append((got, plan["base"]))
    return message, got


def arrived(parts, got):
    for part in parts:
        part.got[-1] = got, part.got[-1][1]


def inputs_grad_kernel(at_ref, own_ref, away_ref, w_ref, out_ref, sent_ref):
    tokens, width = out_ref.shape[0], own_ref.shape[1]
    n = tokens // 8
    for cols in tiles(out_ref.shape[1]):
        value = dot_t(own_ref[:tokens, :], w_ref[cols, :width])
        value = value + dot_t(away_ref[:tokens, :], w_ref[cols, width:])
        for i, away in enumerate(AWAY_Z):
            place = jnp.where((at_ref[2] + at_ref[0]) % 2 == 0, Z_ORDER.index(away % 8), Z_ORDER.index(-away % 8))
            out_ref[pl.ds(pl.multiple_of(place * n, n), n), cols] = value[i * n : (i + 1) * n]
    sent_ref[...] = out_ref[4 * n :, :].astype(BF)


def inputs_grad(at, own, away, w_in):
    rows, cols = own.shape[0] - 16, w_in.shape[0]
    outs = [((rows, cols), F32), ((rows // 2, cols), BF)]
    return local(inputs_grad_kernel, "inputs_grad", outs, at, own, away, w_in)


def rows_kernel(scale, at_ref, keep_ref, got_ref, out_ref):
    for h in range(2):
        here = slice(h * 128, h * 128 + 128)
        there = pl.ds(pl.multiple_of((at_ref[0] ^ h) * 128, 128), 128)
        out_ref[there, :] = (keep_ref[here, :] + got_ref[here, :].astype(F32)) * scale


def place_rows(at, scale, keep, got):
    kernel = functools.partial(rows_kernel, scale)
    return local(kernel, "place_rows", (keep.shape, F32), at, keep, got)


def columns_kernel(scale, at_ref, keep_ref, got_ref, keep2_ref, got2_ref, sent_ref, out_ref, in_ref, bias_ref):
    for h, (k, g) in enumerate(((keep_ref, got_ref), (keep2_ref, got2_ref))):
        for i in range(8):
            at = pl.multiple_of((2 * i + (at_ref[0] ^ h)) * 128, 128)
            cols = slice(i * 128, i * 128 + 128)
            out_ref[:, pl.ds(at, 128)] = (k[:, cols] + g[:128, cols].astype(F32)) * scale
    v = [joined(ref, start) for ref in (sent_ref, got2_ref) for start in (128, 144)]
    zero = at_ref[0] == 0
    first = v[0] + jnp.where(zero, v[1], v[2])
    second = jnp.where(zero, v[2], v[1]) + v[3]
    total = (first + second) * scale
    for i in range(8):
        cols = slice(i * 128, i * 128 + 128)
        for row in range(2):
            in_ref[2 * i + row : 2 * i + row + 1, :] = total[row : row + 1, cols]
        bias_ref[i : i + 1, :] = total[2:3, cols]


def place_columns(at, scale, keep, got, keep2, got2, sent2):
    rows, cols = keep.shape
    kernel = functools.partial(columns_kernel, scale)
    outs = [((rows, 2 * cols), F32), ((16, 128), F32), ((8, 128), F32)]
    return local(kernel, "place_columns", outs, at, keep, got, keep2, got2, sent2)


def body(inputs, w_in, b_in, w_out, cotangent):
    core = lax.axis_index("row") % 2
    total_tokens = inputs.shape[0] * COLS * DEPTHS
    scale = 1.0 / math.sqrt(total_tokens)
    at = jnp.stack([core, lax.axis_index("depth"), lax.axis_index("col")]).astype(jnp.int32)
    n = inputs.shape[0]

    bias = bias_mine(at, b_in)
    w_in, w_in_plain = permute(at, w_in, 1, (place_of, plain_of))
    (w_out,) = permute(at, w_out, 0, (place_of,))
    near = gather_near(pack(inputs, cotangent), bias, w_in_plain, w_out)
    far = gather_far(near)

    tok_near, terms = arrange_near(at, near, w_in)
    chip_near = chip_sum(at, tok_near, w_in, send(terms, CORE), False)
    got_near = send(chip_near, NEAR)
    tok, cot, terms, cot_sum = arrange_far(at, tok_near, near + far, w_in)
    terms_two = grad_other(at, cot, w_out)
    terms, got_near, terms_two = together(send(terms, CORE), got_near, terms_two)
    chip_far = chip_sum(at, tok, w_in, terms, False)
    got_far = send(chip_far, NEAR)
    chip_two = chip_sum(at, cot, w_out, send(after(terms_two, chip_far), CORE), True)
    got_two = send(chip_two, NEAR)
    got_far = after(got_far, chip_two)
    act = gelu(at, (chip_near, got_near), (chip_far, got_far), bias, 0)
    act_away = send(act, CORE)

    out = [DepthSum((OWN,), (act,), cot), DepthSum((AWAY,), (act_away,), cot)]
    got = [exchange(at, [part], Y_ONE)[1] for part in out]
    bias = after(bias, act_away)
    slope = gelu(at, (chip_near, got_near), (chip_far, got_far), bias, 1)
    tok_one, tok_two = by_depth(at, after(tok, slope))
    pg = pre_grad(at, after(slope, tok_one), chip_two, got_two)
    pg_away = send(pg, CORE)

    got[0], got[1], tok_one, tok_two, _ = together(*got, tok_one, tok_two, pg)
    arrived(out[:1], got[0])
    arrived(out[1:], got[1])
    one = DepthSum((OWN,), (tok_one,), pg)
    sent_one, got_one = exchange(at, [*out, one], Y_TWO)
    two = DepthSum((OWN,), (after(tok_two, sent_one),), pg_away, (pg, pg_away, cot_sum))
    sent_two, got_two = exchange(at, [two], X_HI)
    gi, gi_sent = inputs_grad(at, after(pg, sent_two), pg_away, w_in_plain)
    gi_got = [send(gi_sent, Z_STEPS[0])]
    gi_sent = (gi[2 * n : 4 * n] + gi_got[0][2 * n :].astype(F32)).astype(BF)
    gi_got.append(send(gi_sent, Z_STEPS[1]))

    got_one, got_two, gi_got[1] = together(got_one, got_two, gi_got[1])
    arrived([*out, one], got_one)
    arrived([two], got_two)
    sent_one, got_one = exchange(at, [one, two], Y_ONE)
    sent_two, got_two = exchange(at, out, X_HI)
    gi_sent = gi[n : 2 * n] + gi_got[0][n : 2 * n].astype(F32) + gi_got[1][n:].astype(F32)
    gi_sent = gi_sent.astype(BF)
    gi_got.append(send(gi_sent, Z_STEPS[2]))
    out_kept = kept_rows(at, out, sent_one, sent_two, gi_sent)

    got_one, got_two, gi_got[2], out_kept = together(got_one, got_two, gi_got[2], out_kept)
    arrived([one, two], got_one)
    got_out = got_two
    sent_one, got_one = exchange(at, [one], X_HI)
    sent_two, got_two = exchange(at, [two], Y_TWO)
    sent = sent_one, sent_two
    one_kept, two_kept = kept_rows(at, [one], *sent), kept_rows(at, [two], *sent)
    grad_w_out = place_rows(at, scale, after(out_kept, one_kept, two_kept), got_out)
    gi = gi[:n] + sum(got[:n].astype(F32) for got in gi_got)
    grad_inputs = gi.astype(BF)
    grad_w_in, db_in, db_out = place_columns(
        at, scale, one_kept, got_one, two_kept, got_two, sent_two
    )
    grad_b_in, grad_b_out = db_in.reshape(-1), db_out.reshape(-1)
    return (grad_inputs, grad_w_in, grad_b_in, grad_w_out, grad_b_out)


def solution(mesh):
    in_specs = (
        P(("col", "depth"), "row"),
        P("row", "col"),
        P("col"),
        P("col", "row"),
        P(("col", "depth"), "row"),
    )
    out_specs = (
        P(("col", "depth"), "row"),
        P(("row", "depth"), "col"),
        P("col"),
        P(("col", "depth"), "row"),
        P("row"),
    )
    return jax.shard_map(body, mesh=mesh, in_specs=in_specs, out_specs=out_specs, check_vma=False)
```

```python
import functools
import math

import jax
import jax.numpy as jnp
from jax import lax
from jax.experimental import pallas as pl
from jax.experimental.pallas import tpu as pltpu
from jax.sharding import PartitionSpec as P

root_two_pi = 0.7978845608028654
cubic_coef = 0.044715

AXES = ("row", "col", "depth")
COLS, DEPTHS = 8, 8
BF, F32 = jnp.bfloat16, jnp.float32

Y_FIRST = ((0, 1, 6, 7, 2, 3, 4, 5), (0, 1, 2, 3, 6, 7, 4, 5))
X_FIRST = ((0, 6, 2, 4, 1, 7, 3, 5), (0, 2, 6, 4, 1, 3, 7, 5))


def gelu_pair(pre):
    inner = root_two_pi * (pre + cubic_coef * pre * pre * pre)
    tangent = jnp.tanh(inner)
    act = 0.5 * pre * (1.0 + tangent)
    slope = 0.5 * (1.0 + tangent) + 0.5 * pre * (1.0 - tangent * tangent) * root_two_pi * (
        1.0 + 3.0 * cubic_coef * pre * pre
    )
    return (act, slope)


def flat(x, y, z, core):
    row = (x % 2) * 2 + core
    depth = y * 2 + x // 2
    return (row * COLS + z) * DEPTHS + depth


def pairs_of(target):
    pairs = []
    for x in range(4):
        for y in range(4):
            for z in range(8):
                for core in range(2):
                    tx, ty, tz, tc = target(x, y, z, core)
                    pairs.append((flat(x, y, z, core), flat(tx % 4, ty % 4, tz % 8, tc % 2)))
    return pairs


CORE = pairs_of(lambda x, y, z, c: (x, y, z, c ^ 1))
NEAR = pairs_of(lambda x, y, z, c: (x ^ 1, y, z, c))
X_HI = pairs_of(lambda x, y, z, c: (x + 2, y, z, c))
Y_ONE = pairs_of(lambda x, y, z, c: (x, y ^ (3 if c else 1), z, c))
Y_TWO = pairs_of(lambda x, y, z, c: (x, y ^ (1 if c else 3), z, c))
Z = {k: pairs_of(lambda x, y, z, c, k=k: (x, y, z + k, c)) for k in (-2, -1, 1, 2)}
Z_STEPS = [
    pairs_of(lambda x, y, z, c, k=k: (x, y, z + (k if (z + c) % 2 == 0 else -k), c)) for k in (1, -1, 3)
]
Z_ORDER = (0, 3, 7, 4, 1, 6, 2, 5)


def send(value, pairs):
    return lax.ppermute(value, AXES, pairs)


def together(*values):
    return lax.optimization_barrier(values)


def after(value, *others):
    return together(value, *others)[0]


def dot(a, b):
    return jnp.dot(a, b, preferred_element_type=F32)


def dot_t(a, b):
    return lax.dot_general(a, b, (((1,), (1,)), ((), ())), preferred_element_type=F32)


def dot_tn(a, b):
    return lax.dot_general(a, b, (((0,), (0,)), ((), ())), preferred_element_type=F32)


ANY = pl.BlockSpec(memory_space=pl.ANY)
WHOLE = pl.BlockSpec(memory_space=pltpu.VMEM)
SCALARS = pl.BlockSpec(memory_space=pltpu.SMEM)
STEP = 256


def tiles(n):
    return [slice(i, i + STEP) for i in range(0, n, STEP)]


def local(kernel, name, outs, at, *arrays):
    single = not isinstance(outs, list)
    shapes = [jax.ShapeDtypeStruct(*out) for out in ([outs] if single else outs)]
    return pl.pallas_call(
        kernel,
        in_specs=[SCALARS] + [WHOLE] * len(arrays),
        out_specs=WHOLE if single else [WHOLE] * len(shapes),
        out_shape=shapes[0] if single else shapes,
        cost_estimate=pl.CostEstimate(flops=0, bytes_accessed=1 << 12, transcendentals=0),
        compiler_params=pltpu.CompilerParams(vmem_limit_bytes=16 << 20),
        name=name,
    )(at, *arrays)


def order_of(i, at, order=Y_FIRST):
    packed = [sum(k << (4 * j) for j, k in enumerate(ks)) for ks in order]
    return ((jnp.where(at[0] == 0, packed[0], packed[1]) >> (4 * i)) & 7) ^ at[1]


def place_of(i, at):
    h = i // 8
    return order_of(i % 8, (at[0] ^ h, at[1])) * 2 + (at[0] ^ h)


def plain_of(i, at):
    return (i % 8) * 2 + (at[0] ^ (i // 8))


def permute_kernel(axis, orders, at_ref, a_ref, *refs):
    outs, sems = refs[:-1], refs[-1]
    copies = []
    for o, (order, out) in enumerate(zip(orders, outs)):
        for i in range(16):
            source = pl.ds(pl.multiple_of(order(i, at_ref) * 128, 128), 128)
            target = pl.ds(i * 128, 128)
            if axis == 1:
                source, target = (slice(None), source), (slice(None), target)
            copies.append(
                pltpu.make_async_copy(a_ref.at[source], out.at[target], sems.at[16 * o + i])
            )
    for copy in copies:
        copy.start()
    for copy in copies:
        copy.wait()


def permute(at, w, axis, orders):
    return pl.pallas_call(
        functools.partial(permute_kernel, axis, orders),
        in_specs=[SCALARS, ANY],
        out_specs=[WHOLE] * len(orders),
        out_shape=[jax.ShapeDtypeStruct(w.shape, w.dtype)] * len(orders),
        scratch_shapes=[pltpu.SemaphoreType.DMA((16 * len(orders),))],
        compiler_params=pltpu.CompilerParams(vmem_limit_bytes=16 << 20),
        cost_estimate=pl.CostEstimate(flops=0, bytes_accessed=1 << 12, transcendentals=0),
        name=f"permute_{axis}",
    )(at, w)


def bias_kernel(at_ref, b_ref, b_out):
    for i in range(8):
        at = pl.multiple_of(place_of(i, at_ref) * 128, 128)
        b_out[:, i * 128 : (i + 1) * 128] = b_ref[:, pl.ds(at, 128)].astype(F32)


def bias_mine(at, b):
    return local(bias_kernel, "bias_mine", ((1, b.shape[0] // 2), F32), at, b.reshape(1, -1))


def pack_kernel(a_ref, b_ref, out_ref, sems):
    rows = a_ref.shape[0]
    copies = [
        pltpu.make_async_copy(ref, out_ref.at[pl.ds(i * rows, rows)], sems.at[i])
        for i, ref in enumerate((a_ref, b_ref))
    ]
    for copy in copies:
        copy.start()
    for copy in copies:
        copy.wait()


def pack(a, b):
    return pl.pallas_call(
        pack_kernel,
        in_specs=[ANY] * 2,
        out_specs=WHOLE,
        out_shape=jax.ShapeDtypeStruct((2 * a.shape[0], a.shape[1]), a.dtype),
        scratch_shapes=[pltpu.SemaphoreType.DMA((2,))],
        cost_estimate=pl.CostEstimate(flops=0, bytes_accessed=1 << 12, transcendentals=0),
        name="pack",
    )(a, b)


AWAY_Z = (0, 1, 2, -2, -1, 3, -3, 4)
NEAR_BLOCKS = 5


def gather_near(block, *meanwhile):
    found = {k: send(block, Z[-k]) for k in (-1, 1, -2, 2)}
    found = dict(zip(found, together(*found.values(), *meanwhile)))
    return [block] + [found[k] for k in AWAY_Z[1:NEAR_BLOCKS]]


def gather_far(near):
    half = near[0].shape[0] // 2
    up, down = near[2], near[3]
    last = send(up[:half], Z[-2]), send(down[half:], Z[2])
    return [send(up, Z[-1]), send(down, Z[1]), *last]


def arrange_near_kernel(at_ref, *refs):
    blocks, w_ref, tok_out, out_ref = refs[:NEAR_BLOCKS], *refs[NEAR_BLOCKS:]
    n = blocks[0].shape[0] // 2
    for i, block in enumerate(blocks):
        tok_out[i * n : (i + 1) * n, :] = block[:n, :]
    width = out_ref.shape[1]
    for cols in tiles(width):
        other = slice(width + cols.start, width + cols.stop)
        out_ref[:, cols] = dot(tok_out[...], w_ref[:, other]).astype(BF)


def arrange_near(at, blocks, w_in):
    rows, cols = blocks[0].shape
    rows = rows // 2 * NEAR_BLOCKS
    outs = [((rows, cols), BF), ((rows, w_in.shape[1] // 2), BF)]
    return local(arrange_near_kernel, "arrange_near", outs, at, *blocks, w_in)


def arrange_far_kernel(at_ref, tok_ref, *refs):
    blocks, w_ref, tok_out, cot_out, out_ref, sums, sum_out = refs[:9], *refs[9:]
    n = blocks[0].shape[0] // 2
    first = tok_ref.shape[0]
    tok_out[:first, :] = tok_ref[...]
    for i, block in enumerate(blocks[:7]):
        rows = slice(i * n, (i + 1) * n)
        if i >= NEAR_BLOCKS:
            tok_out[rows, :] = block[:n, :]
        cot_out[rows, :] = block[n:, :]
    tok_out[7 * n :, :] = blocks[7][...]
    cot_out[7 * n :, :] = blocks[8][...]
    width = out_ref.shape[1]
    for cols in tiles(width):
        other = slice(width + cols.start, width + cols.stop)
        out_ref[:, cols] = dot(tok_out[first:, :], w_ref[:, other]).astype(BF)
    for i, k in enumerate(AWAY_Z):
        value = jnp.sum(cot_out[i * n : (i + 1) * n, :].astype(F32), axis=0, keepdims=True)
        sums[pl.ds((at_ref[2] + k) & 7, 1), :] = value
    sum_out[...] = jnp.sum(sums[...], axis=0, keepdims=True)


def arrange_far(at, tok, blocks, w_in):
    rows, cols = blocks[0].shape
    rows, width = 4 * rows, w_in.shape[1] // 2
    outs = [((rows, cols), BF)] * 2 + [((rows - tok.shape[0], width), BF), ((8, cols), F32), ((1, cols), F32)]
    tok, cot, terms, _, cot_sum = local(arrange_far_kernel, "arrange_far", outs, at, tok, *blocks, w_in)
    return tok, cot, terms, cot_sum


def grad_other_kernel(at_ref, cot_ref, w_ref, out_ref):
    width = out_ref.shape[1]
    for cols in tiles(width):
        other = slice(width + cols.start, width + cols.stop)
        out_ref[:, cols] = dot_t(cot_ref[...], w_ref[other, :]).astype(BF)


def grad_other(at, cot, w_out):
    out = ((cot.shape[0], w_out.shape[0] // 2), BF)
    return local(grad_other_kernel, "grad_other", out, at, cot, w_out)


def chip_kernel(transposed, at_ref, a_ref, w_ref, got_ref, out_ref):
    rows = slice(a_ref.shape[0] - out_ref.shape[0], a_ref.shape[0])
    for cols in tiles(out_ref.shape[1]):
        if transposed:
            value = dot_t(a_ref[rows, :], w_ref[cols, :])
        else:
            value = dot(a_ref[rows, :], w_ref[:, cols])
        out_ref[:, cols] = (value + got_ref[:, cols].astype(F32)).astype(BF)


def chip_sum(at, a, w, got, transposed):
    kernel = functools.partial(chip_kernel, transposed)
    return local(kernel, "chip_sum", (got.shape, BF), at, a, w, got)


def gelu_kernel(slope, at_ref, *refs):
    halves, bias_ref, out_ref = (refs[:2], refs[2:4]), refs[4], refs[5]
    base = 0
    for chip_ref, got_ref in halves:

        @pl.loop(0, chip_ref.shape[0], step=16)
        def _(i, base=base, chip_ref=chip_ref, got_ref=got_ref):
            i = pl.multiple_of(i, 16)
            rows = pl.ds(i, 16)
            pre = chip_ref[rows, :].astype(F32) + got_ref[rows, :].astype(F32)
            value = gelu_pair(pre + bias_ref[...])[slope]
            out_ref[pl.ds(pl.multiple_of(base + i, 16), 16), :] = value.astype(out_ref.dtype)

        base += chip_ref.shape[0]


def gelu(at, near, far, bias, slope):
    rows = near[0].shape[0] + far[0].shape[0]
    out, name = ((rows, bias.shape[1]), F32 if slope else BF), "slope" if slope else "act"
    return local(functools.partial(gelu_kernel, slope), name, out, at, *near, *far, bias)


def split(value):
    high = value.astype(BF).astype(F32)
    return jnp.concatenate([high, value - high], axis=0).astype(BF)


def joined(ref, start):
    return ref[start : start + 8, :].astype(F32) + ref[start + 8 : start + 16, :].astype(F32)


def pre_grad_kernel(at_ref, slope_ref, chip_ref, got_ref, out_ref):
    tokens = chip_ref.shape[0]
    row = lax.broadcasted_iota(jnp.int32, (8, 128), 0)
    for b in range(8):
        here = slice(b * 128, b * 128 + 128)
        there = pl.ds(pl.multiple_of(order_of(b, at_ref) * 128, 128), 128)
        grad = chip_ref[:, here].astype(F32) + got_ref[:, here].astype(F32)
        value = (slope_ref[:, here] * grad).astype(BF)
        out_ref[:tokens, there] = value
        total = jnp.sum(value.astype(F32), axis=0, keepdims=True)
        out_ref[tokens:, there] = split(jnp.where(row == 0, total, 0.0))


def pre_grad(at, slope, chip, got):
    rows, cols = slope.shape
    return local(pre_grad_kernel, "pre_grad", ((rows + 16, cols), BF), at, slope, chip, got)


def by_depth_kernel(at_ref, a_ref, *outs):
    for order, out in zip((Y_FIRST[::-1], X_FIRST), outs):
        for i in range(8):
            at = pl.multiple_of(order_of(i, at_ref, order) * 128, 128)
            out[:, i * 128 : (i + 1) * 128] = a_ref[:, pl.ds(at, 128)]


def by_depth(at, a):
    return local(by_depth_kernel, "by_depth", [(a.shape, a.dtype)] * 2, at, a)


OWN = (((512, 1024),), ((256, 512),), ((128, 256),), ((0, 128),))
AWAY = (((256, 512), (768, 1024)), ((512, 768),), ((128, 256),), ((0, 128),))


SIZES = (512, 256, 128, 128)


def depth_part(plan, at_ref, refs, out_ref):
    sides, level = plan["sides"], plan["level"]
    lefts = [next(refs) for _ in sides]
    right_ref = next(refs)
    got_refs = [(next(refs), offset) for offset in plan["got"]]
    size, base = SIZES[level], plan["base"]
    skip = 0 if level == 3 else size
    for s, (side, left_ref) in enumerate(zip(sides, lefts)):
        done = 0
        for start, stop in side[level]:
            rows = slice(base + s * size + done, base + s * size + done + stop - start)
            for cols in tiles(out_ref.shape[1]):
                value = dot_tn(left_ref[:, start:stop], right_ref[: left_ref.shape[0], cols])
                for i, (got_ref, offset) in enumerate(got_refs):
                    at = offset + s * SIZES[i] + skip + done
                    value = value + got_ref[at : at + stop - start, cols].astype(F32)
                out_ref[rows, cols] = value.astype(out_ref.dtype)
            done += stop - start
    base += size * len(sides)
    if plan["riders"] == "first":
        own, away, cot_sum = next(refs), next(refs), next(refs)
        row = lax.broadcasted_iota(jnp.int32, (8, out_ref.shape[1]), 0)
        value = jnp.where(row == 2, cot_sum[...], 0.0)
        value = jnp.where(row == at_ref[0], joined(own, own.shape[0] - 16)[:1], value)
        value = jnp.where(row == 1 - at_ref[0], joined(away, away.shape[0] - 16)[:1], value)
        out_ref[base : base + 16, :] = split(value)
    elif plan["riders"] is not None:
        sent, got = next(refs), got_refs[-1]
        here, there = plan["riders"] + SIZES[level - 1], got[1] + SIZES[level - 1]
        if level == 1:
            out_ref[base : base + 16, :] = split(joined(sent, here) + joined(got[0], there))
        else:
            out_ref[base : base + 16, :] = sent[here : here + 16, :]
            out_ref[base + 16 : base + 32, :] = got[0][there : there + 16, :]


def depth_kernel(plans, at_ref, *refs):
    given = iter(refs[:-1])
    for plan in plans:
        depth_part(plan, at_ref, given, refs[-1])


class DepthSum:
    def __init__(self, sides, lefts, right, riders=()):
        self.sides, self.lefts, self.right, self.riders = sides, lefts, right, riders
        self.sent, self.got = [], []

    def plan(self, level, base):
        got, riders, size = self.got[: min(level, 2)], None, SIZES[level] * len(self.sides)
        given = [*self.lefts, self.right, *(message for message, _ in got)]
        if self.riders and level < 3:
            riders = self.sent[-1][1] if level else "first"
            given += [self.sent[-1][0]] if level else self.riders
            size += 32 if level == 2 else 16
        offsets = [offset for _, offset in got]
        return dict(sides=self.sides, level=level, got=offsets, riders=riders, base=base), given, size


def kept_rows(at, parts, *earlier):
    plans, operands, base = [], [], 0
    parts[0].right = after(parts[0].right, *earlier)
    for part in parts:
        plan, given, size = part.plan(3, base)
        plans.append(plan)
        operands += given
        base += size
    out = ((base, parts[0].right.shape[1]), F32)
    return local(functools.partial(depth_kernel, plans), "depth_kept", out, at, *operands)


def exchange(at, parts, pairs):
    plans, operands, base = [], [], 0
    for part in parts:
        plan, given, size = part.plan(len(part.got), base)
        plans.append(plan)
        operands += given
        base += size
    out = ((base, parts[0].right.shape[1]), BF)
    message = local(functools.partial(depth_kernel, plans), "depth", out, at, *operands)
    got = send(message, pairs)
    for part, plan in zip(parts, plans):
        part.sent.append((message, plan["base"]))
        part.got.append((got, plan["base"]))
    return message, got


def arrived(parts, got):
    for part in parts:
        part.got[-1] = got, part.got[-1][1]


def inputs_grad_kernel(at_ref, own_ref, away_ref, w_ref, out_ref, sent_ref):
    tokens, width = out_ref.shape[0], own_ref.shape[1]
    n = tokens // 8
    for cols in tiles(out_ref.shape[1]):
        value = dot_t(own_ref[:tokens, :], w_ref[cols, :width])
        value = value + dot_t(away_ref[:tokens, :], w_ref[cols, width:])
        for i, away in enumerate(AWAY_Z):
            place = jnp.where((at_ref[2] + at_ref[0]) % 2 == 0, Z_ORDER.index(away % 8), Z_ORDER.index(-away % 8))
            out_ref[pl.ds(pl.multiple_of(place * n, n), n), cols] = value[i * n : (i + 1) * n]
    sent_ref[...] = out_ref[4 * n :, :].astype(BF)


def inputs_grad(at, own, away, w_in):
    rows, cols = own.shape[0] - 16, w_in.shape[0]
    outs = [((rows, cols), F32), ((rows // 2, cols), BF)]
    return local(inputs_grad_kernel, "inputs_grad", outs, at, own, away, w_in)


def rows_kernel(scale, at_ref, keep_ref, got_ref, out_ref):
    for h in range(2):
        here = slice(h * 128, h * 128 + 128)
        there = pl.ds(pl.multiple_of((at_ref[0] ^ h) * 128, 128), 128)
        out_ref[there, :] = (keep_ref[here, :] + got_ref[here, :].astype(F32)) * scale


def place_rows(at, scale, keep, got):
    kernel = functools.partial(rows_kernel, scale)
    return local(kernel, "place_rows", (keep.shape, F32), at, keep, got)


def columns_kernel(scale, at_ref, keep_ref, got_ref, keep2_ref, got2_ref, sent_ref, out_ref, in_ref, bias_ref):
    for h, (k, g) in enumerate(((keep_ref, got_ref), (keep2_ref, got2_ref))):
        for i in range(8):
            at = pl.multiple_of((2 * i + (at_ref[0] ^ h)) * 128, 128)
            cols = slice(i * 128, i * 128 + 128)
            out_ref[:, pl.ds(at, 128)] = (k[:, cols] + g[:128, cols].astype(F32)) * scale
    v = [joined(ref, start) for ref in (sent_ref, got2_ref) for start in (128, 144)]
    zero = at_ref[0] == 0
    first = v[0] + jnp.where(zero, v[1], v[2])
    second = jnp.where(zero, v[2], v[1]) + v[3]
    total = (first + second) * scale
    for i in range(8):
        cols = slice(i * 128, i * 128 + 128)
        for row in range(2):
            in_ref[2 * i + row : 2 * i + row + 1, :] = total[row : row + 1, cols]
        bias_ref[i : i + 1, :] = total[2:3, cols]


def place_columns(at, scale, keep, got, keep2, got2, sent2):
    rows, cols = keep.shape
    kernel = functools.partial(columns_kernel, scale)
    outs = [((rows, 2 * cols), F32), ((16, 128), F32), ((8, 128), F32)]
    return local(kernel, "place_columns", outs, at, keep, got, keep2, got2, sent2)


def body(inputs, w_in, b_in, w_out, cotangent):
    core = lax.axis_index("row") % 2
    total_tokens = inputs.shape[0] * COLS * DEPTHS
    scale = 1.0 / math.sqrt(total_tokens)
    at = jnp.stack([core, lax.axis_index("depth"), lax.axis_index("col")]).astype(jnp.int32)
    n = inputs.shape[0]

    bias = bias_mine(at, b_in)
    w_in, w_in_plain = permute(at, w_in, 1, (place_of, plain_of))
    (w_out,) = permute(at, w_out, 0, (place_of,))
    near = gather_near(pack(inputs, cotangent), bias, w_in_plain, w_out)
    far = gather_far(near)

    tok_near, terms = arrange_near(at, near, w_in)
    chip_near = chip_sum(at, tok_near, w_in, send(terms, CORE), False)
    got_near = send(chip_near, NEAR)
    tok, cot, terms, cot_sum = arrange_far(at, tok_near, near + far, w_in)
    terms_two = grad_other(at, cot, w_out)
    terms, got_near, terms_two = together(send(terms, CORE), got_near, terms_two)
    chip_far = chip_sum(at, tok, w_in, terms, False)
    got_far = send(chip_far, NEAR)
    chip_two = chip_sum(at, cot, w_out, send(after(terms_two, chip_far), CORE), True)
    got_two = send(chip_two, NEAR)
    got_far = after(got_far, chip_two)
    act = gelu(at, (chip_near, got_near), (chip_far, got_far), bias, 0)
    act_away = send(act, CORE)

    out = [DepthSum((OWN,), (act,), cot), DepthSum((AWAY,), (act_away,), cot)]
    got = [exchange(at, [part], Y_ONE)[1] for part in out]
    bias = after(bias, act_away)
    slope = gelu(at, (chip_near, got_near), (chip_far, got_far), bias, 1)
    tok_one, tok_two = by_depth(at, after(tok, slope))
    pg = pre_grad(at, after(slope, tok_one), chip_two, got_two)
    pg_away = send(pg, CORE)

    got[0], got[1], tok_one, tok_two, _ = together(*got, tok_one, tok_two, pg)
    arrived(out[:1], got[0])
    arrived(out[1:], got[1])
    one = DepthSum((OWN,), (tok_one,), pg)
    sent_one, got_one = exchange(at, [*out, one], Y_TWO)
    two = DepthSum((OWN,), (after(tok_two, sent_one),), pg_away, (pg, pg_away, cot_sum))
    sent_two, got_two = exchange(at, [two], X_HI)
    gi, gi_sent = inputs_grad(at, after(pg, sent_two), pg_away, w_in_plain)
    gi_got = [send(gi_sent, Z_STEPS[0])]
    gi_sent = (gi[2 * n : 4 * n] + gi_got[0][2 * n :].astype(F32)).astype(BF)
    gi_got.append(send(gi_sent, Z_STEPS[1]))

    got_one, got_two, gi_got[1] = together(got_one, got_two, gi_got[1])
    arrived([*out, one], got_one)
    arrived([two], got_two)
    sent_one, got_one = exchange(at, [one, two], Y_ONE)
    sent_two, got_two = exchange(at, out, X_HI)
    gi_sent = gi[n : 2 * n] + gi_got[0][n : 2 * n].astype(F32) + gi_got[1][n:].astype(F32)
    gi_sent = gi_sent.astype(BF)
    gi_got.append(send(gi_sent, Z_STEPS[2]))
    out_kept = kept_rows(at, out, sent_one, sent_two, gi_sent)

    got_one, got_two, gi_got[2], out_kept = together(got_one, got_two, gi_got[2], out_kept)
    arrived([one, two], got_one)
    got_out = got_two
    sent_one, got_one = exchange(at, [one], X_HI)
    sent_two, got_two = exchange(at, [two], Y_TWO)
    sent = sent_one, sent_two
    one_kept, two_kept = kept_rows(at, [one], *sent), kept_rows(at, [two], *sent)
    grad_w_out = place_rows(at, scale, after(out_kept, one_kept, two_kept), got_out)
    gi = gi[:n] + sum(got[:n].astype(F32) for got in gi_got)
    grad_inputs = gi.astype(BF)
    grad_w_in, db_in, db_out = place_columns(
        at, scale, one_kept, got_one, two_kept, got_two, sent_two
    )
    grad_b_in, grad_b_out = db_in.reshape(-1), db_out.reshape(-1)
    return (grad_inputs, grad_w_in, grad_b_in, grad_w_out, grad_b_out)


def solution(mesh):
    in_specs = (
        P(("col", "depth"), "row"),
        P("row", "col"),
        P("col"),
        P("col", "row"),
        P(("col", "depth"), "row"),
    )
    out_specs = (
        P(("col", "depth"), "row"),
        P(("row", "depth"), "col"),
        P("col"),
        P(("col", "depth"), "row"),
        P("row"),
    )
    return jax.shard_map(body, mesh=mesh, in_specs=in_specs, out_specs=out_specs, check_vma=False)
```

```python
import functools
import math

import jax
import jax.numpy as jnp
from jax import lax
from jax.experimental import pallas as pl
from jax.experimental.pallas import tpu as pltpu
from jax.sharding import PartitionSpec as P

root_two_pi = 0.7978845608028654
cubic_coef = 0.044715

AXES = ("row", "col", "depth")
COLS, DEPTHS = 8, 8
BF, F32 = jnp.bfloat16, jnp.float32

Y_FIRST = ((0, 1, 6, 7, 2, 3, 4, 5), (0, 1, 2, 3, 6, 7, 4, 5))
X_FIRST = ((0, 6, 2, 4, 1, 7, 3, 5), (0, 2, 6, 4, 1, 3, 7, 5))


def gelu_pair(pre):
    inner = root_two_pi * (pre + cubic_coef * pre * pre * pre)
    tangent = jnp.tanh(inner)
    act = 0.5 * pre * (1.0 + tangent)
    slope = 0.5 * (1.0 + tangent) + 0.5 * pre * (1.0 - tangent * tangent) * root_two_pi * (
        1.0 + 3.0 * cubic_coef * pre * pre
    )
    return (act, slope)


def flat(x, y, z, core):
    row = (x % 2) * 2 + core
    depth = y * 2 + x // 2
    return (row * COLS + z) * DEPTHS + depth


def pairs_of(target):
    pairs = []
    for x in range(4):
        for y in range(4):
            for z in range(8):
                for core in range(2):
                    tx, ty, tz, tc = target(x, y, z, core)
                    pairs.append((flat(x, y, z, core), flat(tx % 4, ty % 4, tz % 8, tc % 2)))
    return pairs


CORE = pairs_of(lambda x, y, z, c: (x, y, z, c ^ 1))
NEAR = pairs_of(lambda x, y, z, c: (x ^ 1, y, z, c))
X_HI = pairs_of(lambda x, y, z, c: (x + 2, y, z, c))
Y_ONE = pairs_of(lambda x, y, z, c: (x, y ^ (3 if c else 1), z, c))
Y_TWO = pairs_of(lambda x, y, z, c: (x, y ^ (1 if c else 3), z, c))
Z = {k: pairs_of(lambda x, y, z, c, k=k: (x, y, z + k, c)) for k in (-2, -1, 1, 2)}
Z_STEPS = [
    pairs_of(lambda x, y, z, c, k=k: (x, y, z + (k if (z + c) % 2 == 0 else -k), c)) for k in (1, -1, 3)
]
Z_ORDER = (0, 3, 7, 4, 1, 6, 2, 5)


def send(value, pairs):
    return lax.ppermute(value, AXES, pairs)


def together(*values):
    return lax.optimization_barrier(values)


def after(value, *others):
    return together(value, *others)[0]


def dot(a, b):
    return jnp.dot(a, b, preferred_element_type=F32)


def dot_t(a, b):
    return lax.dot_general(a, b, (((1,), (1,)), ((), ())), preferred_element_type=F32)


def dot_tn(a, b):
    return lax.dot_general(a, b, (((0,), (0,)), ((), ())), preferred_element_type=F32)


ANY = pl.BlockSpec(memory_space=pl.ANY)
WHOLE = pl.BlockSpec(memory_space=pltpu.VMEM)
SCALARS = pl.BlockSpec(memory_space=pltpu.SMEM)
STEP = 256


def tiles(n):
    return [slice(i, i + STEP) for i in range(0, n, STEP)]


def local(kernel, name, outs, at, *arrays):
    single = not isinstance(outs, list)
    shapes = [jax.ShapeDtypeStruct(*out) for out in ([outs] if single else outs)]
    return pl.pallas_call(
        kernel,
        in_specs=[SCALARS] + [WHOLE] * len(arrays),
        out_specs=WHOLE if single else [WHOLE] * len(shapes),
        out_shape=shapes[0] if single else shapes,
        cost_estimate=pl.CostEstimate(flops=0, bytes_accessed=1 << 12, transcendentals=0),
        compiler_params=pltpu.CompilerParams(vmem_limit_bytes=16 << 20),
        name=name,
    )(at, *arrays)


def order_of(i, at, order=Y_FIRST):
    packed = [sum(k << (4 * j) for j, k in enumerate(ks)) for ks in order]
    return ((jnp.where(at[0] == 0, packed[0], packed[1]) >> (4 * i)) & 7) ^ at[1]


def place_of(i, at):
    h = i // 8
    return order_of(i % 8, (at[0] ^ h, at[1])) * 2 + (at[0] ^ h)


def plain_of(i, at):
    return (i % 8) * 2 + (at[0] ^ (i // 8))


def permute_kernel(axis, orders, at_ref, a_ref, *refs):
    outs, sems = refs[:-1], refs[-1]
    copies = []
    for o, (order, out) in enumerate(zip(orders, outs)):
        for i in range(16):
            source = pl.ds(pl.multiple_of(order(i, at_ref) * 128, 128), 128)
            target = pl.ds(i * 128, 128)
            if axis == 1:
                source, target = (slice(None), source), (slice(None), target)
            copies.append(
                pltpu.make_async_copy(a_ref.at[source], out.at[target], sems.at[16 * o + i])
            )
    for copy in copies:
        copy.start()
    for copy in copies:
        copy.wait()


def permute(at, w, axis, orders):
    return pl.pallas_call(
        functools.partial(permute_kernel, axis, orders),
        in_specs=[SCALARS, ANY],
        out_specs=[WHOLE] * len(orders),
        out_shape=[jax.ShapeDtypeStruct(w.shape, w.dtype)] * len(orders),
        scratch_shapes=[pltpu.SemaphoreType.DMA((16 * len(orders),))],
        compiler_params=pltpu.CompilerParams(vmem_limit_bytes=16 << 20),
        cost_estimate=pl.CostEstimate(flops=0, bytes_accessed=1 << 12, transcendentals=0),
        name=f"permute_{axis}",
    )(at, w)


def bias_kernel(at_ref, b_ref, b_out):
    for i in range(8):
        at = pl.multiple_of(place_of(i, at_ref) * 128, 128)
        b_out[:, i * 128 : (i + 1) * 128] = b_ref[:, pl.ds(at, 128)].astype(F32)


def bias_mine(at, b):
    return local(bias_kernel, "bias_mine", ((1, b.shape[0] // 2), F32), at, b.reshape(1, -1))


def pack_kernel(a_ref, b_ref, out_ref, sems):
    rows = a_ref.shape[0]
    copies = [
        pltpu.make_async_copy(ref, out_ref.at[pl.ds(i * rows, rows)], sems.at[i])
        for i, ref in enumerate((a_ref, b_ref))
    ]
    for copy in copies:
        copy.start()
    for copy in copies:
        copy.wait()


def pack(a, b):
    return pl.pallas_call(
        pack_kernel,
        in_specs=[ANY] * 2,
        out_specs=WHOLE,
        out_shape=jax.ShapeDtypeStruct((2 * a.shape[0], a.shape[1]), a.dtype),
        scratch_shapes=[pltpu.SemaphoreType.DMA((2,))],
        cost_estimate=pl.CostEstimate(flops=0, bytes_accessed=1 << 12, transcendentals=0),
        name="pack",
    )(a, b)


AWAY_Z = (0, 1, 2, -2, -1, 3, -3, 4)
NEAR_BLOCKS = 5


def gather_near(block, *meanwhile):
    found = {k: send(block, Z[-k]) for k in (2, -2, 1, -1)}
    found = dict(zip(found, together(*found.values(), *meanwhile)))
    return [block] + [found[k] for k in AWAY_Z[1:NEAR_BLOCKS]]


def gather_far(near):
    half = near[0].shape[0] // 2
    up, down = near[2], near[3]
    last = send(up[:half], Z[-2]), send(down[half:], Z[2])
    return [send(up, Z[-1]), send(down, Z[1]), *last]


def arrange_near_kernel(at_ref, *refs):
    blocks, w_ref, tok_out, out_ref = refs[:NEAR_BLOCKS], *refs[NEAR_BLOCKS:]
    n = blocks[0].shape[0] // 2
    for i, block in enumerate(blocks):
        tok_out[i * n : (i + 1) * n, :] = block[:n, :]
    width = out_ref.shape[1]
    for cols in tiles(width):
        other = slice(width + cols.start, width + cols.stop)
        out_ref[:, cols] = dot(tok_out[...], w_ref[:, other]).astype(BF)


def arrange_near(at, blocks, w_in):
    rows, cols = blocks[0].shape
    rows = rows // 2 * NEAR_BLOCKS
    outs = [((rows, cols), BF), ((rows, w_in.shape[1] // 2), BF)]
    return local(arrange_near_kernel, "arrange_near", outs, at, *blocks, w_in)


def arrange_far_kernel(at_ref, tok_ref, *refs):
    blocks, w_ref, tok_out, cot_out, out_ref, sums, sum_out = refs[:9], *refs[9:]
    n = blocks[0].shape[0] // 2
    first = tok_ref.shape[0]
    tok_out[:first, :] = tok_ref[...]
    for i, block in enumerate(blocks[:7]):
        rows = slice(i * n, (i + 1) * n)
        if i >= NEAR_BLOCKS:
            tok_out[rows, :] = block[:n, :]
        cot_out[rows, :] = block[n:, :]
    tok_out[7 * n :, :] = blocks[7][...]
    cot_out[7 * n :, :] = blocks[8][...]
    width = out_ref.shape[1]
    for cols in tiles(width):
        other = slice(width + cols.start, width + cols.stop)
        out_ref[:, cols] = dot(tok_out[first:, :], w_ref[:, other]).astype(BF)
    for i, k in enumerate(AWAY_Z):
        value = jnp.sum(cot_out[i * n : (i + 1) * n, :].astype(F32), axis=0, keepdims=True)
        sums[pl.ds((at_ref[2] + k) & 7, 1), :] = value
    sum_out[...] = jnp.sum(sums[...], axis=0, keepdims=True)


def arrange_far(at, tok, blocks, w_in):
    rows, cols = blocks[0].shape
    rows, width = 4 * rows, w_in.shape[1] // 2
    outs = [((rows, cols), BF)] * 2 + [((rows - tok.shape[0], width), BF), ((8, cols), F32), ((1, cols), F32)]
    tok, cot, terms, _, cot_sum = local(arrange_far_kernel, "arrange_far", outs, at, tok, *blocks, w_in)
    return tok, cot, terms, cot_sum


def grad_other_kernel(at_ref, cot_ref, w_ref, out_ref):
    width = out_ref.shape[1]
    for cols in tiles(width):
        other = slice(width + cols.start, width + cols.stop)
        out_ref[:, cols] = dot_t(cot_ref[...], w_ref[other, :]).astype(BF)


def grad_other(at, cot, w_out):
    out = ((cot.shape[0], w_out.shape[0] // 2), BF)
    return local(grad_other_kernel, "grad_other", out, at, cot, w_out)


def chip_kernel(transposed, at_ref, a_ref, w_ref, got_ref, out_ref):
    rows = slice(a_ref.shape[0] - out_ref.shape[0], a_ref.shape[0])
    for cols in tiles(out_ref.shape[1]):
        if transposed:
            value = dot_t(a_ref[rows, :], w_ref[cols, :])
        else:
            value = dot(a_ref[rows, :], w_ref[:, cols])
        out_ref[:, cols] = (value + got_ref[:, cols].astype(F32)).astype(BF)


def chip_sum(at, a, w, got, transposed):
    kernel = functools.partial(chip_kernel, transposed)
    return local(kernel, "chip_sum", (got.shape, BF), at, a, w, got)


def gelu_kernel(slope, at_ref, *refs):
    halves, bias_ref, out_ref = (refs[:2], refs[2:4]), refs[4], refs[5]
    base = 0
    for chip_ref, got_ref in halves:

        @pl.loop(0, chip_ref.shape[0], step=16)
        def _(i, base=base, chip_ref=chip_ref, got_ref=got_ref):
            i = pl.multiple_of(i, 16)
            rows = pl.ds(i, 16)
            pre = chip_ref[rows, :].astype(F32) + got_ref[rows, :].astype(F32)
            value = gelu_pair(pre + bias_ref[...])[slope]
            out_ref[pl.ds(pl.multiple_of(base + i, 16), 16), :] = value.astype(out_ref.dtype)

        base += chip_ref.shape[0]


def gelu(at, near, far, bias, slope):
    rows = near[0].shape[0] + far[0].shape[0]
    out, name = ((rows, bias.shape[1]), F32 if slope else BF), "slope" if slope else "act"
    return local(functools.partial(gelu_kernel, slope), name, out, at, *near, *far, bias)


def split(value):
    high = value.astype(BF).astype(F32)
    return jnp.concatenate([high, value - high], axis=0).astype(BF)


def joined(ref, start):
    return ref[start : start + 8, :].astype(F32) + ref[start + 8 : start + 16, :].astype(F32)


def pre_grad_kernel(at_ref, slope_ref, chip_ref, got_ref, out_ref):
    tokens = chip_ref.shape[0]
    row = lax.broadcasted_iota(jnp.int32, (8, 128), 0)
    for b in range(8):
        here = slice(b * 128, b * 128 + 128)
        there = pl.ds(pl.multiple_of(order_of(b, at_ref) * 128, 128), 128)
        grad = chip_ref[:, here].astype(F32) + got_ref[:, here].astype(F32)
        value = (slope_ref[:, here] * grad).astype(BF)
        out_ref[:tokens, there] = value
        total = jnp.sum(value.astype(F32), axis=0, keepdims=True)
        out_ref[tokens:, there] = split(jnp.where(row == 0, total, 0.0))


def pre_grad(at, slope, chip, got):
    rows, cols = slope.shape
    return local(pre_grad_kernel, "pre_grad", ((rows + 16, cols), BF), at, slope, chip, got)


def by_depth_kernel(at_ref, a_ref, *outs):
    for order, out in zip((Y_FIRST[::-1], X_FIRST), outs):
        for i in range(8):
            at = pl.multiple_of(order_of(i, at_ref, order) * 128, 128)
            out[:, i * 128 : (i + 1) * 128] = a_ref[:, pl.ds(at, 128)]


def by_depth(at, a):
    return local(by_depth_kernel, "by_depth", [(a.shape, a.dtype)] * 2, at, a)


OWN = (((512, 1024),), ((256, 512),), ((128, 256),), ((0, 128),))
AWAY = (((256, 512), (768, 1024)), ((512, 768),), ((128, 256),), ((0, 128),))


SIZES = (512, 256, 128, 128)


def depth_part(plan, at_ref, refs, out_ref):
    sides, level = plan["sides"], plan["level"]
    lefts = [next(refs) for _ in sides]
    right_ref = next(refs)
    got_refs = [(next(refs), offset) for offset in plan["got"]]
    size, base = SIZES[level], plan["base"]
    skip = 0 if level == 3 else size
    for s, (side, left_ref) in enumerate(zip(sides, lefts)):
        done = 0
        for start, stop in side[level]:
            rows = slice(base + s * size + done, base + s * size + done + stop - start)
            for cols in tiles(out_ref.shape[1]):
                value = dot_tn(left_ref[:, start:stop], right_ref[: left_ref.shape[0], cols])
                for i, (got_ref, offset) in enumerate(got_refs):
                    at = offset + s * SIZES[i] + skip + done
                    value = value + got_ref[at : at + stop - start, cols].astype(F32)
                out_ref[rows, cols] = value.astype(out_ref.dtype)
            done += stop - start
    base += size * len(sides)
    if plan["riders"] == "first":
        own, away, cot_sum = next(refs), next(refs), next(refs)
        row = lax.broadcasted_iota(jnp.int32, (8, out_ref.shape[1]), 0)
        value = jnp.where(row == 2, cot_sum[...], 0.0)
        value = jnp.where(row == at_ref[0], joined(own, own.shape[0] - 16)[:1], value)
        value = jnp.where(row == 1 - at_ref[0], joined(away, away.shape[0] - 16)[:1], value)
        out_ref[base : base + 16, :] = split(value)
    elif plan["riders"] is not None:
        sent, got = next(refs), got_refs[-1]
        here, there = plan["riders"] + SIZES[level - 1], got[1] + SIZES[level - 1]
        if level == 1:
            out_ref[base : base + 16, :] = split(joined(sent, here) + joined(got[0], there))
        else:
            out_ref[base : base + 16, :] = sent[here : here + 16, :]
            out_ref[base + 16 : base + 32, :] = got[0][there : there + 16, :]


def depth_kernel(plans, at_ref, *refs):
    given = iter(refs[:-1])
    for plan in plans:
        depth_part(plan, at_ref, given, refs[-1])


class DepthSum:
    def __init__(self, sides, lefts, right, riders=()):
        self.sides, self.lefts, self.right, self.riders = sides, lefts, right, riders
        self.sent, self.got = [], []

    def plan(self, level, base):
        got, riders, size = self.got[: min(level, 2)], None, SIZES[level] * len(self.sides)
        given = [*self.lefts, self.right, *(message for message, _ in got)]
        if self.riders and level < 3:
            riders = self.sent[-1][1] if level else "first"
            given += [self.sent[-1][0]] if level else self.riders
            size += 32 if level == 2 else 16
        offsets = [offset for _, offset in got]
        return dict(sides=self.sides, level=level, got=offsets, riders=riders, base=base), given, size


def kept_rows(at, parts, *earlier):
    plans, operands, base = [], [], 0
    parts[0].right = after(parts[0].right, *earlier)
    for part in parts:
        plan, given, size = part.plan(3, base)
        plans.append(plan)
        operands += given
        base += size
    out = ((base, parts[0].right.shape[1]), F32)
    return local(functools.partial(depth_kernel, plans), "depth_kept", out, at, *operands)


def exchange(at, parts, pairs):
    plans, operands, base = [], [], 0
    for part in parts:
        plan, given, size = part.plan(len(part.got), base)
        plans.append(plan)
        operands += given
        base += size
    out = ((base, parts[0].right.shape[1]), BF)
    message = local(functools.partial(depth_kernel, plans), "depth", out, at, *operands)
    got = send(message, pairs)
    for part, plan in zip(parts, plans):
        part.sent.append((message, plan["base"]))
        part.got.append((got, plan["base"]))
    return message, got


def arrived(parts, got):
    for part in parts:
        part.got[-1] = got, part.got[-1][1]


def inputs_grad_kernel(at_ref, own_ref, away_ref, w_ref, out_ref, sent_ref):
    tokens, width = out_ref.shape[0], own_ref.shape[1]
    n = tokens // 8
    for cols in tiles(out_ref.shape[1]):
        value = dot_t(own_ref[:tokens, :], w_ref[cols, :width])
        value = value + dot_t(away_ref[:tokens, :], w_ref[cols, width:])
        for i, away in enumerate(AWAY_Z):
            place = jnp.where((at_ref[2] + at_ref[0]) % 2 == 0, Z_ORDER.index(away % 8), Z_ORDER.index(-away % 8))
            out_ref[pl.ds(pl.multiple_of(place * n, n), n), cols] = value[i * n : (i + 1) * n]
    sent_ref[...] = out_ref[4 * n :, :].astype(BF)


def inputs_grad(at, own, away, w_in):
    rows, cols = own.shape[0] - 16, w_in.shape[0]
    outs = [((rows, cols), F32), ((rows // 2, cols), BF)]
    return local(inputs_grad_kernel, "inputs_grad", outs, at, own, away, w_in)


def rows_kernel(scale, at_ref, keep_ref, got_ref, out_ref):
    for h in range(2):
        here = slice(h * 128, h * 128 + 128)
        there = pl.ds(pl.multiple_of((at_ref[0] ^ h) * 128, 128), 128)
        out_ref[there, :] = (keep_ref[here, :] + got_ref[here, :].astype(F32)) * scale


def place_rows(at, scale, keep, got):
    kernel = functools.partial(rows_kernel, scale)
    return local(kernel, "place_rows", (keep.shape, F32), at, keep, got)


def columns_kernel(scale, at_ref, keep_ref, got_ref, keep2_ref, got2_ref, sent_ref, out_ref, in_ref, bias_ref):
    for h, (k, g) in enumerate(((keep_ref, got_ref), (keep2_ref, got2_ref))):
        for i in range(8):
            at = pl.multiple_of((2 * i + (at_ref[0] ^ h)) * 128, 128)
            cols = slice(i * 128, i * 128 + 128)
            out_ref[:, pl.ds(at, 128)] = (k[:, cols] + g[:128, cols].astype(F32)) * scale
    v = [joined(ref, start) for ref in (sent_ref, got2_ref) for start in (128, 144)]
    zero = at_ref[0] == 0
    first = v[0] + jnp.where(zero, v[1], v[2])
    second = jnp.where(zero, v[2], v[1]) + v[3]
    total = (first + second) * scale
    for i in range(8):
        cols = slice(i * 128, i * 128 + 128)
        for row in range(2):
            in_ref[2 * i + row : 2 * i + row + 1, :] = total[row : row + 1, cols]
        bias_ref[i : i + 1, :] = total[2:3, cols]


def place_columns(at, scale, keep, got, keep2, got2, sent2):
    rows, cols = keep.shape
    kernel = functools.partial(columns_kernel, scale)
    outs = [((rows, 2 * cols), F32), ((16, 128), F32), ((8, 128), F32)]
    return local(kernel, "place_columns", outs, at, keep, got, keep2, got2, sent2)


def body(inputs, w_in, b_in, w_out, cotangent):
    core = lax.axis_index("row") % 2
    total_tokens = inputs.shape[0] * COLS * DEPTHS
    scale = 1.0 / math.sqrt(total_tokens)
    at = jnp.stack([core, lax.axis_index("depth"), lax.axis_index("col")]).astype(jnp.int32)
    n = inputs.shape[0]

    bias = bias_mine(at, b_in)
    w_in, w_in_plain = permute(at, w_in, 1, (place_of, plain_of))
    (w_out,) = permute(at, w_out, 0, (place_of,))
    near = gather_near(pack(inputs, cotangent), bias, w_in_plain, w_out)
    far = gather_far(near)

    tok_near, terms = arrange_near(at, near, w_in)
    chip_near = chip_sum(at, tok_near, w_in, send(terms, CORE), False)
    got_near = send(chip_near, NEAR)
    tok, cot, terms, cot_sum = arrange_far(at, tok_near, near + far, w_in)
    terms_two = grad_other(at, cot, w_out)
    terms, got_near, terms_two = together(send(terms, CORE), got_near, terms_two)
    chip_far = chip_sum(at, tok, w_in, terms, False)
    got_far = send(chip_far, NEAR)
    chip_two = chip_sum(at, cot, w_out, send(after(terms_two, chip_far), CORE), True)
    got_two = send(chip_two, NEAR)
    got_far = after(got_far, chip_two)
    act = gelu(at, (chip_near, got_near), (chip_far, got_far), bias, 0)
    act_away = send(act, CORE)

    out = [DepthSum((OWN,), (act,), cot), DepthSum((AWAY,), (act_away,), cot)]
    got = [exchange(at, [part], Y_ONE)[1] for part in out]
    bias = after(bias, act_away)
    slope = gelu(at, (chip_near, got_near), (chip_far, got_far), bias, 1)
    tok_one, tok_two = by_depth(at, after(tok, slope))
    pg = pre_grad(at, after(slope, tok_one), chip_two, got_two)
    pg_away = send(pg, CORE)

    got[0], got[1], tok_one, tok_two, _ = together(*got, tok_one, tok_two, pg)
    arrived(out[:1], got[0])
    arrived(out[1:], got[1])
    one = DepthSum((OWN,), (tok_one,), pg)
    sent_one, got_one = exchange(at, [*out, one], Y_TWO)
    two = DepthSum((OWN,), (after(tok_two, sent_one),), pg_away, (pg, pg_away, cot_sum))
    sent_two, got_two = exchange(at, [two], X_HI)
    gi, gi_sent = inputs_grad(at, after(pg, sent_two), pg_away, w_in_plain)
    gi_got = [send(gi_sent, Z_STEPS[0])]
    gi_sent = (gi[2 * n : 4 * n] + gi_got[0][2 * n :].astype(F32)).astype(BF)
    gi_got.append(send(gi_sent, Z_STEPS[1]))

    got_one, got_two, gi_got[1] = together(got_one, got_two, gi_got[1])
    arrived([*out, one], got_one)
    arrived([two], got_two)
    sent_one, got_one = exchange(at, [one, two], Y_ONE)
    sent_two, got_two = exchange(at, out, X_HI)
    gi_sent = gi[n : 2 * n] + gi_got[0][n : 2 * n].astype(F32) + gi_got[1][n:].astype(F32)
    gi_sent = gi_sent.astype(BF)
    gi_got.append(send(gi_sent, Z_STEPS[2]))
    out_kept = kept_rows(at, out, sent_one, sent_two, gi_sent)

    got_one, got_two, gi_got[2], out_kept = together(got_one, got_two, gi_got[2], out_kept)
    arrived([one, two], got_one)
    got_out = got_two
    sent_one, got_one = exchange(at, [one], X_HI)
    sent_two, got_two = exchange(at, [two], Y_TWO)
    sent = sent_one, sent_two
    one_kept, two_kept = kept_rows(at, [one], *sent), kept_rows(at, [two], *sent)
    grad_w_out = place_rows(at, scale, after(out_kept, one_kept, two_kept), got_out)
    gi = gi[:n] + sum(got[:n].astype(F32) for got in gi_got)
    grad_inputs = gi.astype(BF)
    grad_w_in, db_in, db_out = place_columns(
        at, scale, one_kept, got_one, two_kept, got_two, sent_two
    )
    grad_b_in, grad_b_out = db_in.reshape(-1), db_out.reshape(-1)
    return (grad_inputs, grad_w_in, grad_b_in, grad_w_out, grad_b_out)


def solution(mesh):
    in_specs = (
        P(("col", "depth"), "row"),
        P("row", "col"),
        P("col"),
        P("col", "row"),
        P(("col", "depth"), "row"),
    )
    out_specs = (
        P(("col", "depth"), "row"),
        P(("row", "depth"), "col"),
        P("col"),
        P(("col", "depth"), "row"),
        P("row"),
    )
    return jax.shard_map(body, mesh=mesh, in_specs=in_specs, out_specs=out_specs, check_vma=False)
```
